256 devices in a mesh: ctx: 16 (over z, y_hi), tp: 16 (over x, y_lo, core).
Axes of the slice: x: 4, y: 4 (y_hi: 2, y_lo: 2; y = y_hi * 2 + y_lo), z: 8, core: 2. Of those that a mesh axis runs over, the one named last changes fastest.
Arguments:
- queries: bfloat16 [4096, 8192], P(('ctx', 'tp')), may hold values from -40 to 40
- keyvals: bfloat16 [4096, 4096], P(('ctx', 'tp')), may hold values from -40 to 40
- cache_kv: bfloat16 [8192, 4096], P('ctx', 'tp'), may hold values from -6 to 6
- conv_input: bfloat16 [4096, 24576], P(('ctx', 'tp')), may hold values from -6 to 6
- gate_input: bfloat16 [4096, 16384], P(('ctx', 'tp')), may hold values from -6 to 6
- dt_raw: bfloat16 [4096, 256], P(('ctx', 'tp')), may hold values from -4 to 4
- conv_weight: float32 [4, 24576], P(None, 'tp'), may hold values from -1.5 to 1.5
- conv_bias: float32 [24576], P('tp'), may hold values from -0.5 to 0.5
- dt_bias: float32 [256], P('tp'), may hold values from -4 to -1
- decay_log: float32 [256], P('tp'), may hold values from -12 to 0
- skip_weight: float32 [256], P('tp'), may hold values from 0.5 to 4
- norm_gain: float32 [16384], P('tp'), may hold values from 0.5 to 1.5
- ssm_init: float32 [256, 64, 256], P('tp'), may hold values from -48 to 48
- conv_init: bfloat16 [3, 24576], P(None, 'tp'), may hold values from -6 to 6
- prompt_start: int32 [1], replicated, may hold values from 8192 to 16384
- cache_length: int32 [1], replicated, may hold values from 512 to 8192
Outputs:
- attn_out: bfloat16 [4096, 8192], P(('ctx', 'tp'))
- mamba_out: bfloat16 [4096, 16384], P(('ctx', 'tp'))
The draws below stay inside these ranges and needn't reach their ends.
All inputs are finite; a program needn't handle non-finite values.
Results may differ from the reference program's by a relative error of at most 0.015.
Values may be sent and summed in bfloat16 or wider, within the bound.
A program may use at most 128 MiB of HBM per device.

```python
import math
import jax
import jax.numpy as jnp
from jax import lax

HEAD = 128
QH_DEV = 4
PHEAD = 64
MH_DEV = 16
STATE = 256
CONV = 4
ROWS = 256
L_DEV = 512
KVH = 16
QH = 64
GROUPS = 16
MHEADS = 256
XW = 1536
PROMPT = 4096
CACHE = 8192
N_CTX = 16


def draw_queries(key, part):
    key = jax.random.fold_in(key, 1)
    values = jnp.clip(jax.random.normal(key, (PROMPT, QH * HEAD), jnp.float32), -6.0, 6.0)
    return values.astype(jnp.bfloat16)


def draw_keyvals(key, part):
    key = jax.random.fold_in(key, 2)
    values = jnp.clip(jax.random.normal(key, (PROMPT, KVH * 2 * HEAD), jnp.float32), -6.0, 6.0)
    return values.astype(jnp.bfloat16)


def draw_decay_log(key, part):
    key = jax.random.fold_in(key, 21)
    slow_share = 0.5
    slow_pick = jax.random.uniform(jax.random.fold_in(key, 1), (MHEADS,), jnp.float32) < slow_share
    slow_rate = jnp.exp(jax.random.uniform(jax.random.fold_in(key, 2), (MHEADS,), jnp.float32, math.log(0.3), math.log(2.0))) / PROMPT / 0.1
    fast_rate = jnp.exp(jax.random.uniform(jax.random.fold_in(key, 3), (MHEADS,), jnp.float32, math.log(1.0 / 50.0), math.log(1.0 / 25.0))) / 0.1
    return jnp.log(jnp.where(slow_pick, slow_rate, fast_rate)).astype(jnp.float32)


def level_of(key, dims, pieces, smallest, largest):
    factor_of, own = 1.0, jax.random.fold_in(key, 6)
    for axis_at, parts in pieces:
        draws = jnp.exp(jax.random.uniform(jax.random.fold_in(own, axis_at), (parts,), jnp.float32, smallest / len(pieces), largest / len(pieces)))
        factor_of = factor_of * jnp.repeat(draws, dims[axis_at] // parts).reshape([-1 if axis == axis_at else 1 for axis in range(len(dims))])
    return factor_of


def scatter_about(rng, extent, scale, most, shards=(), kind=jnp.bfloat16):
    entries = scale * jax.random.normal(rng, extent, jnp.float32)
    if shards:
        entries = entries * level_of(rng, extent, shards, -0.22, 0.18)
    return jnp.clip(entries, -most, most).astype(kind)


def setup_inputs(seed: int = 0) -> dict:
    seeds = jax.random.split(jax.random.key(seed), 17)
    return {
        "queries": draw_queries(jax.random.fold_in(seeds[16], 71), 0),
        "keyvals": draw_keyvals(jax.random.fold_in(seeds[16], 71), 0),
        "cache_kv": scatter_about(seeds[2], (CACHE, KVH * 2 * HEAD), 1.0, 6.0, ((0, 16), (1, 16))),
        "conv_input": scatter_about(seeds[3], (PROMPT, GROUPS * XW), 1.0, 6.0, ((0, 256),)),
        "gate_input": scatter_about(seeds[4], (PROMPT, MHEADS * PHEAD), 1.0, 6.0, ((0, 256),)),
        "dt_raw": scatter_about(seeds[5], (PROMPT, MHEADS), 1.0, 4.0, ((0, 256),)),
        "conv_weight": scatter_about(seeds[6], (CONV, GROUPS * XW), 16 ** -0.5, 1.5, ((1, 16),), jnp.float32),
        "conv_bias": jnp.clip(jax.random.uniform(seeds[7], (GROUPS * XW,), jnp.float32, -0.5, 0.5) * level_of(seeds[7], (GROUPS * XW,), ((0, 16),), -0.4, 0.0), -0.5, 0.5),
        "dt_bias": jnp.clip(-4.0 + 3.0 * jax.random.uniform(seeds[8], (MHEADS,), jnp.float32) ** level_of(seeds[8], (MHEADS,), ((0, 16),), -0.2, 0.2), -4.0, -1.0),
        "decay_log": draw_decay_log(jax.random.fold_in(seeds[16], 71), 0),
        "skip_weight": jnp.clip(0.5 + 3.5 * jax.random.uniform(seeds[10], (MHEADS,), jnp.float32) ** level_of(seeds[10], (MHEADS,), ((0, 16),), -0.2, 0.2), 0.5, 4.0),
        "norm_gain": jnp.clip(1.0 + 0.1 * jax.random.normal(seeds[11], (MHEADS * PHEAD,), jnp.float32), 0.5, 1.5),
        "ssm_init": scatter_about(seeds[12], (MHEADS, PHEAD, STATE), 8.0, 48.0, ((0, 16),), jnp.float32),
        "conv_init": scatter_about(seeds[13], (CONV - 1, GROUPS * XW), 1.0, 6.0, ((1, 16),)),
        "prompt_start": jax.random.randint(seeds[14], (1,), CACHE, 2 * CACHE + 1).astype(jnp.int32),
        "cache_length": jax.random.randint(seeds[15], (1,), L_DEV, CACHE + 1).astype(jnp.int32),
    }


exact_prec = lax.Precision.HIGHEST

def rotate_rows(values, positions, half_width):
    lane_index = jnp.arange(half_width, dtype=jnp.float32)
    inverse = jnp.power(jnp.float32(10000.0), -lane_index / half_width)
    angles = positions.astype(jnp.float32)[:, None] * inverse[None, :]
    cosine = jnp.cos(angles)[:, None, :]
    sine_table = jnp.sin(angles)[:, None, :]
    front_part = values[..., :half_width]
    back_part = values[..., half_width:]
    return jnp.concatenate([front_part * cosine - back_part * sine_table, back_part * cosine + front_part * sine_table], axis=-1)

def blocked(array):
    return array.reshape((N_CTX, ROWS) + array.shape[1:])

def reference(queries, keyvals, cache_kv, conv_input, gate_input, dt_raw, conv_weight, conv_bias, dt_bias, decay_log, skip_weight, norm_gain, ssm_init, conv_init, prompt_start, cache_length):
    half_width = HEAD // 2
    row_index = jnp.arange(PROMPT, dtype=jnp.int32)
    positions = prompt_start[0] + row_index
    query_heads = queries.astype(jnp.float32).reshape(PROMPT, QH, HEAD)
    rot_queries = rotate_rows(query_heads, positions, half_width).astype(jnp.bfloat16)
    prompt_pairs = keyvals.reshape(PROMPT, KVH, 2, HEAD)
    rot_keys = rotate_rows(prompt_pairs[:, :, 0].astype(jnp.float32), positions, half_width).astype(jnp.bfloat16)
    cache_pairs = cache_kv.reshape(CACHE, KVH, 2, HEAD)
    all_keys = jnp.concatenate([cache_pairs[:, :, 0], rot_keys], axis=0).transpose(1, 0, 2)
    all_values = jnp.concatenate([cache_pairs[:, :, 1], prompt_pairs[:, :, 1]], axis=0).transpose(1, 0, 2)
    key_slot = jnp.arange(CACHE + PROMPT, dtype=jnp.int32)
    cache_seen = (key_slot < CACHE) & (key_slot < cache_length[0])
    prompt_key = key_slot - CACHE
    visible = cache_seen[None, :] | (key_slot >= CACHE)[None, :] & (prompt_key[None, :] <= row_index[:, None])
    scale_factor = 1.0 / math.sqrt(HEAD)

    def one_head(inputs):
        head_id, query_rows = inputs
        keys_here = all_keys[head_id // QH_DEV]
        values_here = all_values[head_id // QH_DEV]
        scores = jnp.dot(query_rows, keys_here.T, preferred_element_type=jnp.float32) * scale_factor
        masked = jnp.where(visible, scores, -jnp.inf)
        top_score = lax.optimization_barrier(jnp.max(masked, axis=1, keepdims=True))
        weights = jnp.exp(masked - top_score)
        totals = lax.optimization_barrier(jnp.sum(weights, axis=1, keepdims=True))
        weighted = jnp.dot(weights.astype(jnp.bfloat16), values_here, preferred_element_type=jnp.float32)
        return (weighted / totals).astype(jnp.bfloat16)
    heads_out = lax.map(one_head, (jnp.arange(QH, dtype=jnp.int32), rot_queries.transpose(1, 0, 2)))
    attn_out = heads_out.transpose(1, 0, 2).reshape(PROMPT, QH * HEAD)
    extended = jnp.concatenate([conv_init, conv_input], axis=0).astype(jnp.float32)
    conv_mixed = conv_bias
    for tap_index in range(CONV):
        conv_mixed = conv_mixed + conv_weight[tap_index] * extended[tap_index:tap_index + PROMPT]
    conv_mixed = jax.nn.silu(conv_mixed).reshape(PROMPT, GROUPS, XW)
    inner_width = MH_DEV * PHEAD
    head_inputs = conv_mixed[:, :, :inner_width].reshape(PROMPT, GROUPS, MH_DEV, PHEAD)
    state_in = conv_mixed[:, :, inner_width:inner_width + STATE]
    state_out = conv_mixed[:, :, inner_width + STATE:]
    step_size = jax.nn.softplus(dt_raw.astype(jnp.float32) + dt_bias).reshape(PROMPT, GROUPS, MH_DEV)
    log_decay = -jnp.exp(decay_log).reshape(GROUPS, MH_DEV)[None] * step_size
    local_index = jnp.arange(ROWS, dtype=jnp.int32)
    causal = local_index[:, None] >= local_index[None, :]
    skip_table = skip_weight.reshape(GROUPS, MH_DEV)

    def block_step(carry_state, inputs):
        head_block, input_block, output_block, step_block, log_block = inputs
        cumulative = jnp.cumsum(log_block, axis=0)
        contact = jnp.einsum('tgn,sgn->tsg', output_block, input_block, precision=exact_prec)
        log_gaps = cumulative[:, None] - cumulative[None, :]
        wide_mask = causal[:, :, None, None]
        decays = jnp.where(wide_mask, jnp.exp(jnp.where(wide_mask, log_gaps, 0.0)), 0.0)
        mixing = contact[:, :, :, None] * decays * step_block[None]
        inner_part = jnp.einsum('tsgh,sghp->tghp', mixing, head_block, precision=exact_prec)
        carried_part = jnp.einsum('tgn,ghpn->tghp', output_block, carry_state, precision=exact_prec) * jnp.exp(cumulative)[..., None]
        outputs = inner_part + carried_part + skip_table[None, :, :, None] * head_block
        ending = cumulative[-1]
        towards = jnp.exp(ending[None] - cumulative) * step_block
        fresh_state = jnp.einsum('sgh,sghp,sgn->ghpn', towards, head_block, input_block, precision=exact_prec)
        new_state = jnp.exp(ending)[:, :, None, None] * carry_state + fresh_state
        return (new_state, outputs)
    start_state = ssm_init.reshape(GROUPS, MH_DEV, PHEAD, STATE)
    _, outputs = lax.scan(block_step, start_state, (blocked(head_inputs), blocked(state_in), blocked(state_out), blocked(step_size), blocked(log_decay)))
    y_all = outputs.reshape(PROMPT, GROUPS, inner_width)
    gated = y_all * jax.nn.silu(gate_input.astype(jnp.float32).reshape(PROMPT, GROUPS, inner_width))
    mean_square = lax.optimization_barrier(jnp.mean(gated * gated, axis=-1, keepdims=True))
    normed = gated * lax.rsqrt(mean_square + 1e-05) * norm_gain.reshape(GROUPS, inner_width)
    mamba_out = normed.reshape(PROMPT, MHEADS * PHEAD).astype(jnp.bfloat16)
    return (attn_out, mamba_out)
```

```python
import functools
import math

import jax
import jax.numpy as jnp
from jax import lax
from jax.experimental import pallas as pl
from jax.experimental.pallas import tpu as pltpu
from jax.sharding import PartitionSpec as P

HIGHEST = lax.Precision.HIGHEST
F32 = jnp.float32
BF16 = jnp.bfloat16
MESH = pl.DeviceIdType.MESH
PAD = 16
FLOOR = -1e20
HIDDEN = -1e30


def exact_dot(a, b, dims=(((1,), (0,)), ((), ()))):
    return lax.dot_general(a, b, dims, precision=HIGHEST, preferred_element_type=F32)


def fast_dot(a, b, dims=(((1,), (0,)), ((), ()))):
    return lax.dot_general(a, b, dims, preferred_element_type=F32)


def halves(a):
    high = a.astype(BF16)
    return high, (a - high.astype(F32)).astype(BF16)


def silu(a):
    return a / (1.0 + jnp.exp(-a))


def widened(a, width):
    return jnp.tile(a, (1, -(-width // a.shape[1])))[:, :width]


def kernel(
    n_ctx,
    n_tp,
    phead,
    length_ref,
    q_ref,
    kv_ref,
    cache_ref,
    conv_ref,
    gate_ref,
    dt_ref,
    first_ref,
    tap_ref,
    bias_ref,
    small_ref,
    gain_ref,
    init_ref,
    cos_ref,
    sin_ref,
    attn_ref,
    mamba_ref,
    kvc,
    kvp,
    raw_kv,
    raw_q,
    chan,
    halo,
    gates,
    steps,
    mixed,
    x_high,
    x_low,
    inner,
    grown,
    cum_wide,
    cum_rows,
    contact,
    state_out,
    state_all,
    decay_out,
    decay_all,
    enter_out,
    enter_all,
    queries,
    top,
    acc,
    attn_loc,
    mamba_loc,
    send_sem,
    recv_sem,
    ring_send,
    ring_recv,
    sib_send,
    sib_recv,
):
    c = lax.axis_index("ctx")
    t = lax.axis_index("tp")
    nz = n_ctx // 2
    far = nz // 2
    z = c // 2
    yh = lax.rem(c, 2)
    core = lax.rem(t, 2)
    group = 2 * z + core
    row_part = q_ref.shape[0]
    rows = row_part * n_tp
    q_width = raw_q.shape[1]
    kv_width = raw_kv.shape[1]
    head = kv_width // 2
    local_q = q_width // head
    conv_width = chan.shape[1]
    inner_width = gates.shape[1]
    n_state = (conv_width - inner_width) // 2
    cache_rows = kvc.shape[1]
    my_rows = pl.ds(pl.multiple_of(t * row_part, 16), row_part)
    on_diagonal = yh == core

    def columns(index, width):
        return pl.ds(pl.multiple_of(index * width, 128), width)

    def remote(src, dst, s_sem, r_sem, ctx_id, tp_id):
        return pltpu.make_async_remote_copy(
            src_ref=src,
            dst_ref=dst,
            send_sem=s_sem,
            recv_sem=r_sem,
            device_id=(ctx_id, tp_id),
            device_id_type=MESH,
        )

    def near(src, dst, sem):
        return pltpu.make_async_copy(src, dst, sem)

    def wait_for(ref, sem):
        near(ref, ref, sem).wait()

    barrier = pltpu.get_barrier_semaphore()

    def greet(ctx_id, tp_id):
        pl.semaphore_signal(barrier, inc=1, device_id=(ctx_id, tp_id), device_id_type=MESH)

    def greet_plane(k, carry):
        greet(2 * z + 1 - yh, k)

        @pl.when(k > 0)
        def _():
            greet(c, lax.rem(t + k, n_tp))

        return carry

    lax.fori_loop(0, n_tp, greet_plane, 0)

    def greet_line(k, carry):
        other = lax.rem(z + k, nz)
        greet(2 * other, t)
        greet(2 * other + 1, t)
        return carry

    lax.fori_loop(1, nz, greet_line, 0)
    pl.semaphore_wait(barrier, 2 * n_tp - 1 + 2 * (nz - 1))

    @pl.when(on_diagonal)
    def _():
        near(cache_ref, kvc.at[group], recv_sem.at[5]).start()

    @pl.when(jnp.logical_not(on_diagonal))
    def _():
        remote(
            cache_ref, kvc.at[group_of_partner(z, yh)], send_sem.at[5], recv_sem.at[5], group, t - core + yh
        ).start()

    def send_conv(k, carry):
        p = lax.rem(t + k, n_tp)
        remote(
            conv_ref.at[:, columns(p, conv_width)], chan.at[my_rows], send_sem.at[0], recv_sem.at[0], c, p
        ).start()
        remote(dt_ref, steps.at[my_rows], send_sem.at[1], recv_sem.at[1], c, p).start()
        return carry

    near(conv_ref.at[:, columns(t, conv_width)], chan.at[my_rows], recv_sem.at[0]).start()
    near(dt_ref, steps.at[my_rows], recv_sem.at[1]).start()
    lax.fori_loop(1, n_tp, send_conv, 0)

    def send_heads(src_ref, width, dst_ref, which):
        def body(k, carry):
            h = lax.rem(t + k, n_tp)
            to_ctx = 2 * z + lax.rem(h, 2)
            to_tp = (h // 2) * 2 + yh
            own = jnp.logical_and(to_ctx == c, to_tp == t)
            src = src_ref.at[:, columns(h, width)]
            dst = dst_ref.at[my_rows]

            @pl.when(own)
            def _():
                near(src, dst, recv_sem.at[which]).start()

            @pl.when(jnp.logical_not(own))
            def _():
                remote(src, dst, send_sem.at[which], recv_sem.at[which], to_ctx, to_tp).start()

            return carry

        lax.fori_loop(0, n_tp, body, 0)

    send_heads(kv_ref, kv_width, raw_kv, 2)
    send_heads(q_ref, q_width, raw_q, 3)

    def send_gate(k, carry):
        p = lax.rem(t + k, n_tp)
        remote(
            gate_ref.at[:, columns(p, inner_width)], gates.at[my_rows], send_sem.at[4], recv_sem.at[4], c, p
        ).start()
        return carry

    near(gate_ref.at[:, columns(t, inner_width)], gates.at[my_rows], recv_sem.at[4]).start()
    lax.fori_loop(1, n_tp, send_gate, 0)

    def region(buf, way, dist, parity, cut):
        slot = 2 * lax.rem(z - way * dist + nz, nz) + parity
        if not cut:
            return buf.at[slot]
        half = buf.shape[1] // 2
        return buf.at[slot, pl.ds(0 if way > 0 else half, half)]

    bufs = (kvc, kvp)

    def ring_copy(which, way, step, arriving):
        cut = step + 1 == far
        piece = region(bufs[which], way, step + 1 if arriving else step, core, cut)
        at = (which * 2 + (way < 0)) * far + step
        return remote(
            piece,
            piece,
            ring_send.at[at],
            ring_recv.at[at],
            2 * lax.rem(z + way + nz, nz) + yh,
            t,
        )

    def sib_copy(which, way, dist, arriving):
        cut = dist == far
        piece = region(bufs[which], way, dist, 1 - core if arriving else core, cut)
        at = (which * 2 + (way < 0)) * (far + 1) + dist
        return remote(piece, piece, sib_send.at[at], sib_recv.at[at], c, t + 1 - 2 * core)

    def ring_begin(which):
        for way in (1, -1):
            ring_copy(which, way, 0, False).start()
        sib_copy(which, 1, 0, False).start()

    def ring_advance(which, step):
        for way in (1, -1):
            ring_copy(which, way, step, True).wait_recv()
            if step + 1 < far:
                ring_copy(which, way, step + 1, False).start()
        for way in (1, -1):
            sib_copy(which, way, step + 1, False).start()

    def sib_wait(which, dist):
        for way in (1, -1) if dist else (1,):
            sib_copy(which, way, dist, True).wait_recv()

    wait_for(kvc.at[group], recv_sem.at[5])
    ring_begin(0)

    lane = lax.broadcasted_iota(jnp.int32, (rows, head), 1)
    sine = jnp.where(lane < head // 2, -sin_ref[...], sin_ref[...])
    cosine = cos_ref[...]

    def rotated(a):
        a = a.astype(F32)
        return (a * cosine + pltpu.roll(a, head // 2, 1) * sine).astype(BF16)

    wait_for(chan, recv_sem.at[0])
    halo_copy = remote(
        chan.at[pl.ds(rows - PAD, PAD)], halo, send_sem.at[6], recv_sem.at[6], lax.rem(c + 1, n_ctx), t
    )
    halo_copy.start()
    wait_for(raw_kv, recv_sem.at[2])
    kvp[group] = jnp.concatenate([rotated(raw_kv[:, :head]), raw_kv[:, head:]], axis=1)
    ring_begin(1)
    halo_copy.wait_recv()
    n_taps = tap_ref.shape[0]
    piece = 256

    def convolve(j, carry):
        cols = columns(j, piece)
        before = jnp.where(c == 0, first_ref[:, cols].astype(F32), halo[:, cols].astype(F32))
        wide = jnp.concatenate([before, chan[:, cols].astype(F32)], axis=0)
        total = bias_ref[:, cols]
        for tap in range(n_taps):
            start = PAD - (n_taps - 1) + tap
            total = total + tap_ref[pl.ds(tap, 1), cols] * wide[start : start + rows]
        mixed[:, cols] = silu(total)
        return carry

    lax.fori_loop(0, conv_width // piece, convolve, 0)
    ring_advance(0, 0)

    wait_for(steps, recv_sem.at[1])
    n_heads = inner_width // phead
    all_heads = steps.shape[1]
    pick = lax.broadcasted_iota(jnp.int32, (all_heads, 128), 0) == (
        t * n_heads + lax.broadcasted_iota(jnp.int32, (all_heads, 128), 1)
    )
    raw_step = fast_dot(steps[...], pick.astype(F32).astype(BF16)) + small_ref[0:1, :]
    step_size = jnp.maximum(raw_step, 0.0) + jnp.log1p(jnp.exp(-jnp.abs(raw_step)))
    log_decay = -jnp.exp(small_ref[1:2, :]) * step_size
    row_at = lax.broadcasted_iota(jnp.int32, (rows, rows), 0)
    col_at = lax.broadcasted_iota(jnp.int32, (rows, rows), 1)
    causal = row_at >= col_at
    cumulative = exact_dot(causal.astype(F32), log_decay)
    cum_rows[...] = cumulative.T
    wide_at = 2 * 128

    def states(j, carry):
        cols = columns(j, wide_at)
        spread = lax.broadcasted_iota(jnp.int32, (128, wide_at), 0) == (
            j * (wide_at // phead) + lax.broadcasted_iota(jnp.int32, (128, wide_at), 1) // phead
        )
        spread = spread.astype(F32)
        cum_here = exact_dot(cumulative, spread)
        scaled = mixed[:, cols] * exact_dot(step_size, spread)
        cum_wide[:, cols] = cum_here
        grown[:, cols] = jnp.exp(cum_here)
        high, low = halves(scaled)
        x_high[:, cols] = high
        x_low[:, cols] = low
        inner[:, cols] = mixed[:, cols] * exact_dot(small_ref[2:3, :], spread)
        last = cum_here[rows - 1 : rows]
        toward = scaled * jnp.exp(last - cum_here)
        fresh = exact_dot(mixed[:, pl.ds(inner_width, n_state)], toward, (((0,), (0,)), ((), ())))
        state_out[:, cols] = fresh.astype(BF16)
        decay_out[:, cols] = jnp.broadcast_to(jnp.exp(last), (8, wide_at))
        return carry

    lax.fori_loop(0, inner_width // wide_at, states, 0)

    half_state = n_state // 2

    def share(i):
        return pl.ds(pl.multiple_of(lax.rem(i, 2) * half_state, 16), half_state), columns(i // 2, 128)

    def send_state(k, carry):
        i = lax.rem(c + k, n_ctx)
        some_rows, some_cols = share(i)
        remote(
            decay_out.at[:, some_cols], decay_all.at[c], send_sem.at[8], recv_sem.at[8], i, t
        ).start()
        remote(
            state_out.at[some_rows, some_cols], state_all.at[c], send_sem.at[7], recv_sem.at[7], i, t
        ).start()
        return carry

    own_rows, own_cols = share(c)
    near(decay_out.at[:, own_cols], decay_all.at[c], recv_sem.at[8]).start()
    near(state_out.at[own_rows, own_cols], state_all.at[c], recv_sem.at[7]).start()
    lax.fori_loop(1, n_ctx, send_state, 0)
    ring_advance(1, 0)
    ring_advance(0, 1)

    contact[...] = exact_dot(
        mixed[:, pl.ds(inner_width + n_state, n_state)],
        mixed[:, pl.ds(inner_width, n_state)],
        (((1,), (1,)), ((), ())),
    )
    pair_lane = lax.broadcasted_iota(jnp.int32, (rows, 128), 1)

    def within(j, carry):
        cols = columns(j, 128)
        cum_pair = cum_wide[:, cols]
        both = jnp.concatenate([x_high[:, cols], x_low[:, cols]], axis=1)
        parts = []
        for k in range(2):
            gap = cum_pair[:, k * phead : k * phead + 1] - cum_rows[pl.ds(2 * j + k, 1), :]
            mixing = contact[...] * jnp.exp(jnp.where(causal, gap, HIDDEN))
            high, low = halves(mixing)
            product = fast_dot(high, both)
            parts.append(product[:, :128] + product[:, 128:] + fast_dot(low, both[:, :128]))
        inner[:, cols] = inner[:, cols] + jnp.where(pair_lane < phead, parts[0], parts[1])
        return carry

    lax.fori_loop(0, inner_width // 128, within, 0)
    ring_advance(1, 1)
    ring_advance(0, 2)

    wait_for(decay_all, recv_sem.at[8])
    wait_for(state_all, recv_sem.at[7])

    def scan_group(i, state):
        enter_out[i] = state.astype(BF16)
        return decay_all[i][0:1, :] * state + state_all[i].astype(F32)

    lax.fori_loop(0, n_ctx, scan_group, init_ref[...])

    def send_enter(k, carry):
        i = lax.rem(c + k, n_ctx)
        remote(
            enter_out.at[i], enter_all.at[own_rows, own_cols], send_sem.at[9], recv_sem.at[9], i, t
        ).start()
        return carry

    near(enter_out.at[c], enter_all.at[own_rows, own_cols], recv_sem.at[9]).start()
    lax.fori_loop(1, n_ctx, send_enter, 0)
    ring_advance(1, 2)
    ring_advance(0, 3)
    ring_advance(1, 3)

    wait_for(raw_q, recv_sem.at[3])
    mark = (lax.broadcasted_iota(jnp.int32, (rows, head), 1) == 0).astype(F32).astype(BF16)
    for h in range(local_q):
        part = rotated(raw_q[:, h * head : (h + 1) * head])
        queries[pl.ds(h * rows, rows), :] = jnp.concatenate([part, mark], axis=1)
    top[...] = jnp.full(top.shape, FLOOR, F32)
    acc[...] = jnp.zeros(acc.shape, F32)
    factor = math.log2(math.e) / math.sqrt(head)
    length = length_ref[0]

    def update(key, value, diagonal):
        for h in range(local_q):
            at = pl.ds(h * rows, rows)
            query = queries[at, :] if key.shape[1] > head else queries[at, :head]
            score = fast_dot(query, key, (((1,), (1,)), ((), ())))
            if diagonal:
                score = jnp.where(causal, score, HIDDEN)
            old = top[at, :]
            new = jnp.maximum(old, jnp.max(score, axis=1, keepdims=True))
            top[at, :] = new
            weight = jnp.exp2((score - widened(new, score.shape[1])) * factor)
            scale = jnp.exp2((old - new) * factor)
            acc[at, :] = acc[at, :] * widened(scale, 2 * head) + fast_dot(weight.astype(BF16), value)

    def attend_cache(slot):
        lanes = lax.broadcasted_iota(jnp.int32, (cache_rows, head), 1)
        place = slot * cache_rows + lax.broadcasted_iota(jnp.int32, (cache_rows, head), 0)
        hide = jnp.where(jnp.logical_and(lanes == 0, place >= length), HIDDEN, 0.0).astype(BF16)
        block = kvc[slot]
        ones = jnp.ones((cache_rows, head), BF16)
        update(
            jnp.concatenate([block[:, :head], hide], axis=1),
            jnp.concatenate([block[:, head:], ones], axis=1),
            False,
        )

    def attend_prompt(slot):
        def run(diagonal):
            block = kvp[slot]
            ones = jnp.ones((rows, head), BF16)
            update(block[:, :head], jnp.concatenate([block[:, head:], ones], axis=1), diagonal)

        pl.when(slot < group)(functools.partial(run, False))
        pl.when(slot == group)(functools.partial(run, True))

    def attend(k, carry):
        attend_cache(k)
        attend_prompt(k)
        return carry

    for dist in range(far + 1):
        sib_wait(0, dist)
        sib_wait(1, dist)
    lax.fori_loop(0, n_ctx, attend, 0)
    for h in range(local_q):
        found = acc[pl.ds(h * rows, rows), :]
        attn_loc[:, h * head : (h + 1) * head] = (found[:, :head] / found[:, head:]).astype(BF16)

    def send_attn(p, carry):
        src = attn_loc.at[pl.ds(pl.multiple_of(p * row_part, 16), row_part)]
        dst = attn_ref.at[:, columns(t - core + yh, q_width)]
        own = jnp.logical_and(group == c, p == t)

        @pl.when(own)
        def _():
            near(src, dst, recv_sem.at[10]).start()

        @pl.when(jnp.logical_not(own))
        def _():
            remote(src, dst, send_sem.at[10], recv_sem.at[10], group, p).start()

        return carry

    lax.fori_loop(0, n_tp, send_attn, 0)

    wait_for(enter_all, recv_sem.at[9])
    wait_for(gates, recv_sem.at[4])
    out_high, out_low = halves(mixed[:, pl.ds(inner_width + n_state, n_state)])

    def finish(j, squares):
        cols = columns(j, wide_at)
        entering = enter_all[:, cols]
        carried = fast_dot(out_high, entering) + fast_dot(out_low, entering)
        y = inner[:, cols] + grown[:, cols] * carried
        gated = y * silu(gates[:, cols].astype(F32))
        inner[:, cols] = gated
        return squares + jnp.sum(gated * gated, axis=1, keepdims=True)

    squares = lax.fori_loop(0, inner_width // wide_at, finish, jnp.zeros((rows, 1), F32))
    norm = lax.rsqrt(squares / inner_width + 1e-05)

    def normed(j, carry):
        cols = columns(j, wide_at)
        mamba_loc[:, cols] = (inner[:, cols] * norm * gain_ref[:, cols]).astype(BF16)
        return carry

    lax.fori_loop(0, inner_width // wide_at, normed, 0)

    def send_mamba(k, carry):
        p = lax.rem(t + k, n_tp)
        remote(
            mamba_loc.at[pl.ds(pl.multiple_of(p * row_part, 16), row_part)],
            mamba_ref.at[:, columns(t, inner_width)],
            send_sem.at[11],
            recv_sem.at[11],
            c,
            p,
        ).start()
        return carry

    near(mamba_loc.at[my_rows], mamba_ref.at[:, columns(t, inner_width)], recv_sem.at[11]).start()
    lax.fori_loop(1, n_tp, send_mamba, 0)

    wait_for(attn_ref, recv_sem.at[10])
    wait_for(mamba_ref, recv_sem.at[11])
    others = (n_tp - 1) * row_part
    wait_for(chan.at[pl.ds(0, others)], send_sem.at[0])
    wait_for(steps.at[pl.ds(0, others)], send_sem.at[1])
    wait_for(gates.at[pl.ds(0, others)], send_sem.at[4])
    wait_for(mamba_loc.at[pl.ds(0, others)], send_sem.at[11])
    for ref, which in ((raw_kv, 2), (raw_q, 3), (attn_loc, 10)):

        @pl.when(on_diagonal)
        def _(ref=ref, which=which):
            wait_for(ref.at[pl.ds(0, others)], send_sem.at[which])

        @pl.when(jnp.logical_not(on_diagonal))
        def _(ref=ref, which=which):
            wait_for(ref, send_sem.at[which])

    @pl.when(jnp.logical_not(on_diagonal))
    def _():
        wait_for(cache_ref, send_sem.at[5])

    halo_copy.wait_send()
    wait_for(state_all.at[pl.ds(0, n_ctx - 1)], send_sem.at[7])
    wait_for(decay_all.at[pl.ds(0, n_ctx - 1)], send_sem.at[8])
    wait_for(enter_out.at[pl.ds(0, n_ctx - 1)], send_sem.at[9])
    for which in range(2):
        for way in (1, -1):
            for step in range(far):
                ring_copy(which, way, step, False).wait_send()
        sib_copy(which, 1, 0, False).wait_send()
        for dist in range(1, far + 1):
            for way in (1, -1):
                sib_copy(which, way, dist, False).wait_send()


def group_of_partner(z, yh):
    return 2 * z + yh


def local(
    queries,
    keyvals,
    cache_kv,
    conv_input,
    gate_input,
    dt_raw,
    conv_weight,
    conv_bias,
    dt_bias,
    decay_log,
    skip_weight,
    norm_gain,
    ssm_init,
    conv_init,
    prompt_start,
    cache_length,
):
    n_ctx = lax.axis_size("ctx")
    n_tp = lax.axis_size("tp")
    c = lax.axis_index("ctx")
    t = lax.axis_index("tp")
    head = cache_kv.shape[1] // 2
    row_part = queries.shape[0]
    rows = row_part * n_tp
    n_heads, phead, n_state = ssm_init.shape
    inner_width = n_heads * phead
    conv_width = conv_weight.shape[1]
    q_width = queries.shape[1] // n_tp
    cache_rows = cache_kv.shape[0]
    far = n_ctx // 4

    group = (c // 2) * 2 + t % 2
    half_width = head // 2
    lane_index = (jnp.arange(head, dtype=jnp.int32) % half_width).astype(F32)
    inverse = jnp.power(F32(10000.0), -lane_index / half_width)
    positions = prompt_start[0] + group * rows + jnp.arange(rows, dtype=jnp.int32)
    angles = positions.astype(F32)[:, None] * inverse[None, :]
    small = jnp.pad(jnp.stack([dt_bias, decay_log, skip_weight]), ((0, 5), (0, 128 - n_heads)))
    pair = 128 // phead
    init = lax.dynamic_slice(
        ssm_init, ((c // 2) * pair, 0, (c % 2) * (n_state // 2)), (pair, phead, n_state // 2)
    )
    init = init.reshape(pair * phead, n_state // 2).T
    first = jnp.pad(conv_init, ((PAD - conv_init.shape[0], 0), (0, 0)))

    hbm = pl.BlockSpec(memory_space=pl.ANY)
    vmem = pl.BlockSpec(memory_space=pltpu.VMEM)
    smem = pl.BlockSpec(memory_space=pltpu.SMEM)
    dma = pltpu.SemaphoreType.DMA
    local_rows = rows * q_width // head
    return pl.pallas_call(
        functools.partial(kernel, n_ctx, n_tp, phead),
        out_shape=(
            jax.ShapeDtypeStruct(queries.shape, BF16),
            jax.ShapeDtypeStruct(gate_input.shape, BF16),
        ),
        in_specs=[smem] + [hbm] * 6 + [vmem] * 8,
        out_specs=(hbm, hbm),
        scratch_shapes=[
            pltpu.VMEM((n_ctx, cache_rows, 2 * head), BF16),
            pltpu.VMEM((n_ctx, rows, 2 * head), BF16),
            pltpu.VMEM((rows, 2 * head), BF16),
            pltpu.VMEM((rows, q_width), BF16),
            pltpu.VMEM((rows, conv_width), BF16),
            pltpu.VMEM((PAD, conv_width), BF16),
            pltpu.VMEM((rows, inner_width), BF16),
            pltpu.VMEM((rows, dt_raw.shape[1]), BF16),
            pltpu.VMEM((rows, conv_width), F32),
            pltpu.VMEM((rows, inner_width), BF16),
            pltpu.VMEM((rows, inner_width), BF16),
            pltpu.VMEM((rows, inner_width), F32),
            pltpu.VMEM((rows, inner_width), F32),
            pltpu.VMEM((rows, inner_width), F32),
            pltpu.VMEM((128, rows), F32),
            pltpu.VMEM((rows, rows), F32),
            pltpu.VMEM((n_state, inner_width), BF16),
            pltpu.VMEM((n_ctx, n_state // 2, 128), BF16),
            pltpu.VMEM((8, inner_width), F32),
            pltpu.VMEM((n_ctx, 8, 128), F32),
            pltpu.VMEM((n_ctx, n_state // 2, 128), BF16),
            pltpu.VMEM((n_state, inner_width), BF16),
            pltpu.VMEM((local_rows, 2 * head), BF16),
            pltpu.VMEM((local_rows, 128), F32),
            pltpu.VMEM((local_rows, 2 * head), F32),
            pltpu.VMEM((rows, q_width), BF16),
            pltpu.VMEM((rows, inner_width), BF16),
            dma((12,)),
            dma((12,)),
            dma((4 * far,)),
            dma((4 * far,)),
            dma((4 * (far + 1),)),
            dma((4 * (far + 1),)),
        ],
        compiler_params=pltpu.CompilerParams(
            collective_id=0, has_side_effects=True, vmem_limit_bytes=48 * 1024 * 1024
        ),
        cost_estimate=pl.CostEstimate(
            flops=8 * 10**9, bytes_accessed=6 * 10**6, transcendentals=14 * 10**6
        ),
    )(
        cache_length,
        queries,
        keyvals,
        cache_kv,
        conv_input,
        gate_input,
        dt_raw,
        first,
        conv_weight,
        conv_bias[None, :],
        small,
        norm_gain[None, :],
        init,
        jnp.cos(angles),
        jnp.sin(angles),
    )


def solution(mesh):
    return jax.shard_map(
        local,
        mesh=mesh,
        in_specs=(
            P(("ctx", "tp"), None),
            P(("ctx", "tp"), None),
            P("ctx", "tp"),
            P(("ctx", "tp"), None),
            P(("ctx", "tp"), None),
            P(("ctx", "tp"), None),
            P(None, "tp"),
            P("tp"),
            P("tp"),
            P("tp"),
            P("tp"),
            P("tp"),
            P("tp", None, None),
            P(None, "tp"),
            P(),
            P(),
        ),
        out_specs=(P(("ctx", "tp"), None), P(("ctx", "tp"), None)),
        check_vma=False,
    )
```

```python
import functools
import math

import jax
import jax.numpy as jnp
from jax import lax
from jax.experimental import pallas as pl
from jax.experimental.pallas import tpu as pltpu
from jax.sharding import PartitionSpec as P

HIGHEST = lax.Precision.HIGHEST
F32 = jnp.float32
BF16 = jnp.bfloat16
MESH = pl.DeviceIdType.MESH
PAD = 16
FLOOR = -1e20
HIDDEN = -1e30


def exact_dot(a, b, dims=(((1,), (0,)), ((), ()))):
    return lax.dot_general(a, b, dims, precision=HIGHEST, preferred_element_type=F32)


def fast_dot(a, b, dims=(((1,), (0,)), ((), ()))):
    return lax.dot_general(a, b, dims, preferred_element_type=F32)


def halves(a):
    high = a.astype(BF16)
    return high, (a - high.astype(F32)).astype(BF16)


def silu(a):
    return a / (1.0 + jnp.exp(-a))


def widened(a, width):
    return jnp.tile(a, (1, -(-width // a.shape[1])))[:, :width]


def kernel(
    n_ctx,
    n_tp,
    phead,
    length_ref,
    q_ref,
    kv_ref,
    cache_ref,
    conv_ref,
    gate_ref,
    dt_ref,
    init_ref,
    first_ref,
    tap_ref,
    bias_ref,
    dt_bias_ref,
    rate_ref,
    skip_ref,
    gain_ref,
    cos_ref,
    sin_ref,
    attn_ref,
    mamba_ref,
    kvc,
    kvp,
    raw_kv,
    raw_q,
    chan,
    halo,
    gates,
    steps,
    mixed,
    x_high,
    x_low,
    inner,
    grown,
    cum_wide,
    cum_rows,
    contact,
    state_out,
    state_all,
    enter_out,
    enter_all,
    queries,
    top,
    acc,
    attn_loc,
    mamba_loc,
    first,
    small_ref,
    init_piece,
    send_sem,
    recv_sem,
    ring_send,
    ring_recv,
    sib_send,
    sib_recv,
):
    c = lax.axis_index("ctx")
    t = lax.axis_index("tp")
    nz = n_ctx // 2
    far = nz // 2
    z = c // 2
    yh = lax.rem(c, 2)
    core = lax.rem(t, 2)
    group = 2 * z + core
    row_part = q_ref.shape[0]
    rows = row_part * n_tp
    q_width = raw_q.shape[1]
    kv_width = raw_kv.shape[1]
    head = kv_width // 2
    local_q = q_width // head
    conv_width = chan.shape[1]
    inner_width = gates.shape[1]
    n_state = (conv_width - inner_width) // 2
    cache_rows = kvc.shape[1]
    my_rows = pl.ds(pl.multiple_of(t * row_part, 16), row_part)
    on_diagonal = yh == core

    def columns(index, width):
        return pl.ds(pl.multiple_of(index * width, 128), width)

    def remote(src, dst, s_sem, r_sem, ctx_id, tp_id):
        return pltpu.make_async_remote_copy(
            src_ref=src,
            dst_ref=dst,
            send_sem=s_sem,
            recv_sem=r_sem,
            device_id=(ctx_id, tp_id),
            device_id_type=MESH,
        )

    def near(src, dst, sem):
        return pltpu.make_async_copy(src, dst, sem)

    def wait_for(ref, sem):
        near(ref, ref, sem).wait()

    barrier = pltpu.get_barrier_semaphore()

    def greet(ctx_id, tp_id):
        pl.semaphore_signal(barrier, inc=1, device_id=(ctx_id, tp_id), device_id_type=MESH)

    def greet_plane(k, carry):
        greet(2 * z + 1 - yh, k)

        @pl.when(k > 0)
        def _():
            greet(c, lax.rem(t + k, n_tp))

        return carry

    lax.fori_loop(0, n_tp, greet_plane, 0)

    def greet_line(k, carry):
        other = lax.rem(z + k, nz)
        greet(2 * other, t)
        greet(2 * other + 1, t)
        return carry

    lax.fori_loop(1, nz, greet_line, 0)
    pl.semaphore_wait(barrier, 2 * n_tp - 1 + 2 * (nz - 1))

    half_state = n_state // 2
    own_rows = pl.ds(pl.multiple_of(lax.rem(c, 2) * half_state, 128), half_state)
    own_cols = columns(c // 2, 128)
    pair = 128 // phead
    init_copy = near(
        init_ref.at[pl.ds((c // 2) * pair, pair), :, own_rows], init_piece, recv_sem.at[8]
    )
    init_copy.start()

    @pl.when(on_diagonal)
    def _():
        near(cache_ref, kvc.at[group], recv_sem.at[5]).start()

    @pl.when(jnp.logical_not(on_diagonal))
    def _():
        remote(
            cache_ref, kvc.at[group_of_partner(z, yh)], send_sem.at[5], recv_sem.at[5], group, t - core + yh
        ).start()

    def send_heads(src_ref, width, dst_ref, which):
        def body(k, carry):
            h = lax.rem(t + k, n_tp)
            to_ctx = 2 * z + lax.rem(h, 2)
            to_tp = (h // 2) * 2 + yh
            own = jnp.logical_and(to_ctx == c, to_tp == t)
            src = src_ref.at[:, columns(h, width)]
            dst = dst_ref.at[my_rows]

            @pl.when(own)
            def _():
                near(src, dst, recv_sem.at[which]).start()

            @pl.when(jnp.logical_not(own))
            def _():
                remote(src, dst, send_sem.at[which], recv_sem.at[which], to_ctx, to_tp).start()

            return carry

        lax.fori_loop(0, n_tp, body, 0)

    def send_conv(k, carry):
        p = lax.rem(t + k, n_tp)
        remote(
            conv_ref.at[:, columns(p, conv_width)], chan.at[my_rows], send_sem.at[0], recv_sem.at[0], c, p
        ).start()
        remote(dt_ref, steps.at[my_rows], send_sem.at[1], recv_sem.at[1], c, p).start()
        return carry

    def send_gate(k, carry):
        p = lax.rem(t + k, n_tp)
        remote(
            gate_ref.at[:, columns(p, inner_width)], gates.at[my_rows], send_sem.at[4], recv_sem.at[4], c, p
        ).start()
        return carry

    send_heads(kv_ref, kv_width, raw_kv, 2)
    lax.fori_loop(1, n_tp, send_conv, 0)
    near(conv_ref.at[:, columns(t, conv_width)], chan.at[my_rows], recv_sem.at[0]).start()
    near(dt_ref, steps.at[my_rows], recv_sem.at[1]).start()

    def region(buf, way, dist, parity, cut):
        slot = 2 * lax.rem(z - way * dist + nz, nz) + parity
        if not cut:
            return buf.at[slot]
        half = buf.shape[1] // 2
        return buf.at[slot, pl.ds(0 if way > 0 else half, half)]

    bufs = (kvc, kvp)

    def ring_copy(which, way, step, arriving):
        cut = step + 1 == far
        piece = region(bufs[which], way, step + 1 if arriving else step, core, cut)
        at = (which * 2 + (way < 0)) * far + step
        return remote(
            piece,
            piece,
            ring_send.at[at],
            ring_recv.at[at],
            2 * lax.rem(z + way + nz, nz) + yh,
            t,
        )

    def sib_copy(which, way, dist, arriving):
        cut = dist == far
        piece = region(bufs[which], way, dist, 1 - core if arriving else core, cut)
        at = (which * 2 + (way < 0)) * (far + 1) + dist
        return remote(piece, piece, sib_send.at[at], sib_recv.at[at], c, t + 1 - 2 * core)

    def ring_begin(which):
        for way in (1, -1):
            ring_copy(which, way, 0, False).start()
        sib_copy(which, 1, 0, False).start()

    def ring_advance(which, step):
        for way in (1, -1):
            ring_copy(which, way, step, True).wait_recv()
            if step + 1 < far:
                ring_copy(which, way, step + 1, False).start()
        for way in (1, -1):
            sib_copy(which, way, step + 1, False).start()

    def sib_wait(which, dist):
        for way in (1, -1) if dist else (1,):
            sib_copy(which, way, dist, True).wait_recv()

    wait_for(kvc.at[group], recv_sem.at[5])
    ring_begin(0)

    lane = lax.broadcasted_iota(jnp.int32, (rows, head), 1)
    sine = jnp.where(lane < head // 2, -sin_ref[...], sin_ref[...])
    cosine = cos_ref[...]

    def rotated(a):
        a = a.astype(F32)
        return (a * cosine + pltpu.roll(a, head // 2, 1) * sine).astype(BF16)

    wait_for(raw_kv, recv_sem.at[2])
    kvp[group] = jnp.concatenate([rotated(raw_kv[:, :head]), raw_kv[:, head:]], axis=1)
    ring_begin(1)
    ring_advance(0, 0)
    ring_advance(1, 0)
    ring_advance(0, 1)

    wait_for(chan, recv_sem.at[0])
    halo_copy = remote(
        chan.at[pl.ds(rows - PAD, PAD)], halo, send_sem.at[6], recv_sem.at[6], lax.rem(c + 1, n_ctx), t
    )
    halo_copy.start()
    send_heads(q_ref, q_width, raw_q, 3)
    first[...] = jnp.zeros(first.shape, F32)
    first[pl.ds(PAD - first_ref.shape[0], first_ref.shape[0]), :] = first_ref[...].astype(F32)
    n_heads = dt_bias_ref.shape[1]
    small_ref[...] = jnp.zeros(small_ref.shape, F32)
    small_ref[0:1, 0:n_heads] = dt_bias_ref[...]
    small_ref[1:2, 0:n_heads] = rate_ref[...]
    small_ref[2:3, 0:n_heads] = skip_ref[...]
    halo_copy.wait_recv()
    n_taps = tap_ref.shape[0]
    piece = 256

    def convolve(j, carry):
        cols = columns(j, piece)
        before = jnp.where(c == 0, first[:, cols], halo[:, cols].astype(F32))
        wide = jnp.concatenate([before, chan[:, cols].astype(F32)], axis=0)
        total = bias_ref[cols][None, :]
        for tap in range(n_taps):
            start = PAD - (n_taps - 1) + tap
            total = total + tap_ref[pl.ds(tap, 1), cols] * wide[start : start + rows]
        mixed[:, cols] = silu(total)
        return carry

    lax.fori_loop(0, conv_width // piece, convolve, 0)
    ring_advance(1, 1)

    wait_for(steps, recv_sem.at[1])
    all_heads = steps.shape[1]
    pick = lax.broadcasted_iota(jnp.int32, (all_heads, 128), 0) == (
        t * n_heads + lax.broadcasted_iota(jnp.int32, (all_heads, 128), 1)
    )
    raw_step = fast_dot(steps[...], pick.astype(F32).astype(BF16)) + small_ref[0:1, :]
    step_size = jnp.maximum(raw_step, 0.0) + jnp.log1p(jnp.exp(-jnp.abs(raw_step)))
    log_decay = -jnp.exp(small_ref[1:2, :]) * step_size
    row_at = lax.broadcasted_iota(jnp.int32, (rows, rows), 0)
    col_at = lax.broadcasted_iota(jnp.int32, (rows, rows), 1)
    causal = row_at >= col_at
    cumulative = exact_dot(causal.astype(F32), log_decay)
    cum_rows[...] = cumulative.T
    wide_at = 2 * 128

    def states(k, carry):
        j = lax.rem(k + z // 2, inner_width // wide_at)
        cols = columns(j, wide_at)
        spread = lax.broadcasted_iota(jnp.int32, (128, wide_at), 0) == (
            j * (wide_at // phead) + lax.broadcasted_iota(jnp.int32, (128, wide_at), 1) // phead
        )
        spread = spread.astype(F32)
        cum_here = exact_dot(cumulative, spread)
        scaled = mixed[:, cols] * exact_dot(step_size, spread)
        cum_wide[:, cols] = cum_here
        grown[:, cols] = jnp.exp(cum_here)
        high, low = halves(scaled)
        x_high[:, cols] = high
        x_low[:, cols] = low
        inner[:, cols] = mixed[:, cols] * exact_dot(small_ref[2:3, :], spread)
        last = cum_here[rows - 1 : rows]
        toward = scaled * jnp.exp(last - cum_here)
        fresh = exact_dot(mixed[:, pl.ds(inner_width, n_state)], toward, (((0,), (0,)), ((), ())))
        fresh = fresh.astype(BF16)
        decay = jnp.exp(last)
        decay_1 = decay.astype(BF16).astype(F32)
        decay_2 = (decay - decay_1).astype(BF16).astype(F32)
        decay_3 = decay - decay_1 - decay_2
        at = lax.broadcasted_iota(jnp.int32, (PAD, wide_at), 0)
        decays = jnp.where(at == 0, decay_1, jnp.where(at == 1, decay_2, jnp.where(at == 2, decay_3, 0.0)))
        decays = decays.astype(BF16)
        for k in range(2 * wide_at // 128):
            i = j * (2 * wide_at // 128) + k
            lanes = slice(k // 2 * 128, k // 2 * 128 + 128)
            start = k % 2 * half_state
            state_out[i, :half_state] = fresh[start : start + half_state, lanes]
            state_out[i, half_state:] = decays[:, lanes]

            @pl.when(i == c)
            def _(i=i):
                near(state_out.at[i], state_all.at[c], recv_sem.at[7]).start()

            @pl.when(i != c)
            def _(i=i):
                remote(state_out.at[i], state_all.at[c], send_sem.at[7], recv_sem.at[7], i, t).start()

        return carry

    lax.fori_loop(0, inner_width // wide_at, states, 0)

    ring_advance(0, 2)
    ring_advance(1, 2)
    near(gate_ref.at[:, columns(t, inner_width)], gates.at[my_rows], recv_sem.at[4]).start()
    lax.fori_loop(1, n_tp, send_gate, 0)

    contact[...] = exact_dot(
        mixed[:, pl.ds(inner_width + n_state, n_state)],
        mixed[:, pl.ds(inner_width, n_state)],
        (((1,), (1,)), ((), ())),
    )
    pair_lane = lax.broadcasted_iota(jnp.int32, (rows, 128), 1)

    def within(j, carry):
        cols = columns(j, 128)
        cum_pair = cum_wide[:, cols]
        both = jnp.concatenate([x_high[:, cols], x_low[:, cols]], axis=1)
        parts = []
        for k in range(2):
            gap = cum_pair[:, k * phead : k * phead + 1] - cum_rows[pl.ds(2 * j + k, 1), :]
            mixing = contact[...] * jnp.exp(jnp.where(causal, gap, HIDDEN))
            high, low = halves(mixing)
            product = fast_dot(high, both)
            parts.append(product[:, :128] + product[:, 128:] + fast_dot(low, both[:, :128]))
        inner[:, cols] = inner[:, cols] + jnp.where(pair_lane < phead, parts[0], parts[1])
        return carry

    lax.fori_loop(0, inner_width // 128, within, 0)
    ring_advance(0, 3)
    ring_advance(1, 3)

    wait_for(raw_q, recv_sem.at[3])
    mark = (lax.broadcasted_iota(jnp.int32, (rows, head), 1) == 0).astype(F32).astype(BF16)
    for h in range(local_q):
        part = rotated(raw_q[:, h * head : (h + 1) * head])
        queries[pl.ds(h * rows, rows), :] = jnp.concatenate([part, mark], axis=1)
    top[...] = jnp.full(top.shape, FLOOR, F32)
    acc[...] = jnp.zeros(acc.shape, F32)
    factor = math.log2(math.e) / math.sqrt(head)
    length = length_ref[0]
    pair_rows = 2 * cache_rows

    def update(key, value, diagonal):
        for h in range(local_q):
            at = pl.ds(h * rows, rows)
            score = fast_dot(queries[at, :], key, (((1,), (1,)), ((), ())))
            if diagonal:
                shape = (rows, 2 * rows)
                seen = lax.broadcasted_iota(jnp.int32, shape, 1) <= (
                    core * rows + lax.broadcasted_iota(jnp.int32, shape, 0)
                )
                masked = jnp.where(seen, score[:, pair_rows:], HIDDEN)
                score = jnp.concatenate([score[:, :pair_rows], masked], axis=1)
            old = top[at, :]
            new = jnp.maximum(old, jnp.max(score, axis=1, keepdims=True))
            top[at, :] = new
            weight = jnp.exp2((score - widened(new, score.shape[1])) * factor)
            scale = jnp.exp2((old - new) * factor)
            acc[at, :] = acc[at, :] * widened(scale, 2 * head) + fast_dot(weight.astype(BF16), value)

    def attend(place):
        def run(prompt, diagonal):
            lanes = lax.broadcasted_iota(jnp.int32, (pair_rows, head), 1)
            slots = place * pair_rows + lax.broadcasted_iota(jnp.int32, (pair_rows, head), 0)
            hide = jnp.where(jnp.logical_and(lanes == 0, slots >= length), HIDDEN, 0.0).astype(BF16)
            block = kvc[pl.ds(2 * place, 2)].reshape(pair_rows, 2 * head)
            key, value = block[:, :head], block[:, head:]
            if prompt:
                more = kvp[pl.ds(2 * place, 2)].reshape(2 * rows, 2 * head)
                key = jnp.concatenate([key, more[:, :head]], axis=0)
                value = jnp.concatenate([value, more[:, head:]], axis=0)
                hide = jnp.concatenate([hide, jnp.zeros((2 * rows, head), BF16)], axis=0)
            ones = jnp.ones(value.shape, BF16)
            update(
                jnp.concatenate([key, hide], axis=1), jnp.concatenate([value, ones], axis=1), diagonal
            )

        pl.when(place < z)(functools.partial(run, True, False))
        pl.when(place == z)(functools.partial(run, True, True))
        pl.when(place > z)(functools.partial(run, False, False))

    def attend_some(begin, end):
        def body(k, carry):
            attend(lax.rem(z + lax.rem(k, 2) * ((k + 1) // 2) + (1 - lax.rem(k, 2)) * (nz - k // 2), nz))
            return carry

        lax.fori_loop(begin, end, body, 0)

    for dist in range(2):
        sib_wait(0, dist)
        sib_wait(1, dist)
    attend_some(0, 3)

    wait_for(state_all, recv_sem.at[7])
    init_copy.wait()

    def scan_group(i, state):
        enter_out[i] = state.astype(BF16)
        parts = state_all[i, half_state:].astype(F32)
        decay = parts[0:1] + parts[1:2] + parts[2:3]
        return decay * state + state_all[i, :half_state].astype(F32)

    lax.fori_loop(0, n_ctx, scan_group, init_piece[...].reshape(128, half_state).T)

    def send_enter(k, carry):
        i = lax.rem(c + k, n_ctx)
        remote(
            enter_out.at[i], enter_all.at[own_rows, own_cols], send_sem.at[9], recv_sem.at[9], i, t
        ).start()
        return carry

    near(enter_out.at[c], enter_all.at[own_rows, own_cols], recv_sem.at[9]).start()
    lax.fori_loop(1, n_ctx, send_enter, 0)

    for dist in range(2, far + 1):
        sib_wait(0, dist)
        sib_wait(1, dist)
    attend_some(3, nz)
    for h in range(local_q):
        found = acc[pl.ds(h * rows, rows), :]
        attn_loc[:, h * head : (h + 1) * head] = (found[:, :head] / found[:, head:]).astype(BF16)

    def send_attn(p, carry):
        src = attn_loc.at[pl.ds(pl.multiple_of(p * row_part, 16), row_part)]
        dst = attn_ref.at[:, columns(t - core + yh, q_width)]
        own = jnp.logical_and(group == c, p == t)

        @pl.when(own)
        def _():
            near(src, dst, recv_sem.at[10]).start()

        @pl.when(jnp.logical_not(own))
        def _():
            remote(src, dst, send_sem.at[10], recv_sem.at[10], group, p).start()

        return carry

    lax.fori_loop(0, n_tp, send_attn, 0)

    wait_for(enter_all, recv_sem.at[9])
    wait_for(gates, recv_sem.at[4])
    out_high, out_low = halves(mixed[:, pl.ds(inner_width + n_state, n_state)])

    def finish(j, squares):
        cols = columns(j, wide_at)
        entering = enter_all[:, cols]
        carried = fast_dot(out_high, entering) + fast_dot(out_low, entering)
        y = inner[:, cols] + grown[:, cols] * carried
        gated = y * silu(gates[:, cols].astype(F32))
        inner[:, cols] = gated
        return squares + jnp.sum(gated * gated, axis=1, keepdims=True)

    squares = lax.fori_loop(0, inner_width // wide_at, finish, jnp.zeros((rows, 1), F32))
    norm = lax.rsqrt(squares / inner_width + 1e-05)

    def normed(j, carry):
        cols = columns(j, wide_at)
        mamba_loc[:, cols] = (inner[:, cols] * norm * gain_ref[:, cols]).astype(BF16)
        return carry

    lax.fori_loop(0, inner_width // wide_at, normed, 0)

    def send_mamba(k, carry):
        p = lax.rem(t + k, n_tp)
        remote(
            mamba_loc.at[pl.ds(pl.multiple_of(p * row_part, 16), row_part)],
            mamba_ref.at[:, columns(t, inner_width)],
            send_sem.at[11],
            recv_sem.at[11],
            c,
            p,
        ).start()
        return carry

    near(mamba_loc.at[my_rows], mamba_ref.at[:, columns(t, inner_width)], recv_sem.at[11]).start()
    lax.fori_loop(1, n_tp, send_mamba, 0)

    wait_for(attn_ref, recv_sem.at[10])
    wait_for(mamba_ref, recv_sem.at[11])
    others = (n_tp - 1) * row_part
    wait_for(chan.at[pl.ds(0, others)], send_sem.at[0])
    wait_for(steps.at[pl.ds(0, others)], send_sem.at[1])
    wait_for(gates.at[pl.ds(0, others)], send_sem.at[4])
    wait_for(mamba_loc.at[pl.ds(0, others)], send_sem.at[11])
    for ref, which in ((raw_kv, 2), (raw_q, 3), (attn_loc, 10)):

        @pl.when(on_diagonal)
        def _(ref=ref, which=which):
            wait_for(ref.at[pl.ds(0, others)], send_sem.at[which])

        @pl.when(jnp.logical_not(on_diagonal))
        def _(ref=ref, which=which):
            wait_for(ref, send_sem.at[which])

    @pl.when(jnp.logical_not(on_diagonal))
    def _():
        wait_for(cache_ref, send_sem.at[5])

    halo_copy.wait_send()
    wait_for(state_all.at[pl.ds(0, n_ctx - 1)], send_sem.at[7])
    wait_for(enter_out.at[pl.ds(0, n_ctx - 1)], send_sem.at[9])
    for which in range(2):
        for way in (1, -1):
            for step in range(far):
                ring_copy(which, way, step, False).wait_send()
        sib_copy(which, 1, 0, False).wait_send()
        for dist in range(1, far + 1):
            for way in (1, -1):
                sib_copy(which, way, dist, False).wait_send()


def group_of_partner(z, yh):
    return 2 * z + yh


def local(
    queries,
    keyvals,
    cache_kv,
    conv_input,
    gate_input,
    dt_raw,
    conv_weight,
    conv_bias,
    dt_bias,
    decay_log,
    skip_weight,
    norm_gain,
    ssm_init,
    conv_init,
    prompt_start,
    cache_length,
):
    n_ctx = lax.axis_size("ctx")
    n_tp = lax.axis_size("tp")
    c = lax.axis_index("ctx")
    t = lax.axis_index("tp")
    head = cache_kv.shape[1] // 2
    row_part = queries.shape[0]
    rows = row_part * n_tp
    n_heads, phead, n_state = ssm_init.shape
    inner_width = n_heads * phead
    conv_width = conv_weight.shape[1]
    q_width = queries.shape[1] // n_tp
    cache_rows = cache_kv.shape[0]
    far = n_ctx // 4

    group = (c // 2) * 2 + t % 2
    half_width = head // 2
    lane_index = (jnp.arange(head, dtype=jnp.int32) % half_width).astype(F32)
    inverse = jnp.power(F32(10000.0), -lane_index / half_width)
    positions = prompt_start[0] + group * rows + jnp.arange(rows, dtype=jnp.int32)
    angles = positions.astype(F32)[:, None] * inverse[None, :]
    hbm = pl.BlockSpec(memory_space=pl.ANY)
    vmem = pl.BlockSpec(memory_space=pltpu.VMEM)
    smem = pl.BlockSpec(memory_space=pltpu.SMEM)
    dma = pltpu.SemaphoreType.DMA
    local_rows = rows * q_width // head
    return pl.pallas_call(
        functools.partial(kernel, n_ctx, n_tp, phead),
        out_shape=(
            jax.ShapeDtypeStruct(queries.shape, BF16),
            jax.ShapeDtypeStruct(gate_input.shape, BF16),
        ),
        in_specs=[smem] + [hbm] * 7 + [vmem] * 9,
        out_specs=(hbm, hbm),
        scratch_shapes=[
            pltpu.VMEM((n_ctx, cache_rows, 2 * head), BF16),
            pltpu.VMEM((n_ctx, rows, 2 * head), BF16),
            pltpu.VMEM((rows, 2 * head), BF16),
            pltpu.VMEM((rows, q_width), BF16),
            pltpu.VMEM((rows, conv_width), BF16),
            pltpu.VMEM((PAD, conv_width), BF16),
            pltpu.VMEM((rows, inner_width), BF16),
            pltpu.VMEM((rows, dt_raw.shape[1]), BF16),
            pltpu.VMEM((rows, conv_width), F32),
            pltpu.VMEM((rows, inner_width), BF16),
            pltpu.VMEM((rows, inner_width), BF16),
            pltpu.VMEM((rows, inner_width), F32),
            pltpu.VMEM((rows, inner_width), F32),
            pltpu.VMEM((rows, inner_width), F32),
            pltpu.VMEM((128, rows), F32),
            pltpu.VMEM((rows, rows), F32),
            pltpu.VMEM((n_ctx, n_state // 2 + PAD, 128), BF16),
            pltpu.VMEM((n_ctx, n_state // 2 + PAD, 128), BF16),
            pltpu.VMEM((n_ctx, n_state // 2, 128), BF16),
            pltpu.VMEM((n_state, inner_width), BF16),
            pltpu.VMEM((local_rows, 2 * head), BF16),
            pltpu.VMEM((local_rows, 128), F32),
            pltpu.VMEM((local_rows, 2 * head), F32),
            pltpu.VMEM((rows, q_width), BF16),
            pltpu.VMEM((rows, inner_width), BF16),
            pltpu.VMEM((PAD, conv_width), F32),
            pltpu.VMEM((8, 128), F32),
            pltpu.VMEM((128 // phead, phead, n_state // 2), F32),
            dma((12,)),
            dma((12,)),
            dma((4 * far,)),
            dma((4 * far,)),
            dma((4 * (far + 1),)),
            dma((4 * (far + 1),)),
        ],
        compiler_params=pltpu.CompilerParams(
            collective_id=0, has_side_effects=True, vmem_limit_bytes=62 * 1024 * 1024
        ),
        cost_estimate=pl.CostEstimate(
            flops=8 * 10**9, bytes_accessed=6 * 10**6, transcendentals=14 * 10**6
        ),
    )(
        cache_length,
        queries,
        keyvals,
        cache_kv,
        conv_input,
        gate_input,
        dt_raw,
        ssm_init,
        conv_init,
        conv_weight,
        conv_bias,
        dt_bias[None, :],
        decay_log[None, :],
        skip_weight[None, :],
        norm_gain[None, :],
        jnp.cos(angles),
        jnp.sin(angles),
    )


def solution(mesh):
    return jax.shard_map(
        local,
        mesh=mesh,
        in_specs=(
            P(("ctx", "tp"), None),
            P(("ctx", "tp"), None),
            P("ctx", "tp"),
            P(("ctx", "tp"), None),
            P(("ctx", "tp"), None),
            P(("ctx", "tp"), None),
            P(None, "tp"),
            P("tp"),
            P("tp"),
            P("tp"),
            P("tp"),
            P("tp"),
            P("tp", None, None),
            P(None, "tp"),
            P(),
            P(),
        ),
        out_specs=(P(("ctx", "tp"), None), P(("ctx", "tp"), None)),
        check_vma=False,
    )
```

```python
import functools
import math

import jax
import jax.numpy as jnp
from jax import lax
from jax.experimental import pallas as pl
from jax.experimental.pallas import tpu as pltpu
from jax.sharding import PartitionSpec as P

HIGHEST = lax.Precision.HIGHEST
F32 = jnp.float32
BF16 = jnp.bfloat16
MESH = pl.DeviceIdType.MESH
PAD = 16
FLOOR = -1e20
HIDDEN = -1e30


def exact_dot(a, b, dims=(((1,), (0,)), ((), ()))):
    return lax.dot_general(a, b, dims, precision=HIGHEST, preferred_element_type=F32)


def fast_dot(a, b, dims=(((1,), (0,)), ((), ()))):
    return lax.dot_general(a, b, dims, preferred_element_type=F32)


def halves(a):
    high = a.astype(BF16)
    return high, (a - high.astype(F32)).astype(BF16)


def silu(a):
    return a / (1.0 + jnp.exp(-a))


def widened(a, width):
    return jnp.tile(a, (1, -(-width // a.shape[1])))[:, :width]


def kernel(
    n_ctx,
    n_tp,
    phead,
    length_ref,
    q_ref,
    kv_ref,
    cache_ref,
    conv_ref,
    gate_ref,
    dt_ref,
    init_ref,
    first_ref,
    tap_ref,
    bias_ref,
    dt_bias_ref,
    rate_ref,
    skip_ref,
    gain_ref,
    cos_ref,
    sin_ref,
    attn_ref,
    mamba_ref,
    kvc,
    kvp,
    raw_kv,
    raw_q,
    chan,
    halo,
    gates,
    steps,
    mixed,
    x_high,
    x_low,
    inner,
    grown,
    cum_wide,
    step_wide,
    toward_wide,
    skip_wide,
    cum_rows,
    contact,
    state_out,
    state_all,
    enter_out,
    enter_all,
    queries,
    top,
    acc,
    attn_loc,
    mamba_loc,
    first,
    small_ref,
    init_piece,
    send_sem,
    recv_sem,
    ring_send,
    ring_recv,
    sib_send,
    sib_recv,
):
    c = lax.axis_index("ctx")
    t = lax.axis_index("tp")
    nz = n_ctx // 2
    far = nz // 2
    z = c // 2
    yh = lax.rem(c, 2)
    core = lax.rem(t, 2)
    group = 2 * z + core
    row_part = q_ref.shape[0]
    rows = row_part * n_tp
    q_width = raw_q.shape[1]
    kv_width = raw_kv.shape[1]
    head = kv_width // 2
    local_q = q_width // head
    conv_width = chan.shape[1]
    inner_width = gates.shape[1]
    n_state = (conv_width - inner_width) // 2
    cache_rows = kvc.shape[1]
    my_rows = pl.ds(pl.multiple_of(t * row_part, 16), row_part)
    on_diagonal = yh == core

    def columns(index, width):
        return pl.ds(pl.multiple_of(index * width, 128), width)

    def remote(src, dst, s_sem, r_sem, ctx_id, tp_id):
        return pltpu.make_async_remote_copy(
            src_ref=src,
            dst_ref=dst,
            send_sem=s_sem,
            recv_sem=r_sem,
            device_id=(ctx_id, tp_id),
            device_id_type=MESH,
        )

    def near(src, dst, sem):
        return pltpu.make_async_copy(src, dst, sem)

    def wait_for(ref, sem):
        near(ref, ref, sem).wait()

    barrier = pltpu.get_barrier_semaphore()

    def greet(ctx_id, tp_id):
        pl.semaphore_signal(barrier, inc=1, device_id=(ctx_id, tp_id), device_id_type=MESH)

    def greet_plane(k, carry):
        greet(2 * z + 1 - yh, k)

        @pl.when(k > 0)
        def _():
            greet(c, lax.rem(t + k, n_tp))

        return carry

    lax.fori_loop(0, n_tp, greet_plane, 0)

    def greet_line(k, carry):
        other = lax.rem(z + k, nz)
        greet(2 * other, t)
        greet(2 * other + 1, t)
        return carry

    lax.fori_loop(1, nz, greet_line, 0)
    pl.semaphore_wait(barrier, 2 * n_tp - 1 + 2 * (nz - 1))

    half_state = n_state // 2
    own_rows = pl.ds(pl.multiple_of(lax.rem(c, 2) * half_state, 128), half_state)
    own_cols = columns(c // 2, 128)
    pair = 128 // phead
    init_copy = near(
        init_ref.at[pl.ds((c // 2) * pair, pair), :, own_rows], init_piece, recv_sem.at[8]
    )
    init_copy.start()

    @pl.when(on_diagonal)
    def _():
        near(cache_ref, kvc.at[group], recv_sem.at[5]).start()

    @pl.when(jnp.logical_not(on_diagonal))
    def _():
        remote(
            cache_ref, kvc.at[group_of_partner(z, yh)], send_sem.at[5], recv_sem.at[5], group, t - core + yh
        ).start()

    def send_heads(src_ref, width, dst_ref, which):
        def body(k, carry):
            h = lax.rem(t + k, n_tp)
            to_ctx = 2 * z + lax.rem(h, 2)
            to_tp = (h // 2) * 2 + yh
            own = jnp.logical_and(to_ctx == c, to_tp == t)
            src = src_ref.at[:, columns(h, width)]
            dst = dst_ref.at[my_rows]

            @pl.when(own)
            def _():
                near(src, dst, recv_sem.at[which]).start()

            @pl.when(jnp.logical_not(own))
            def _():
                remote(src, dst, send_sem.at[which], recv_sem.at[which], to_ctx, to_tp).start()

            return carry

        lax.fori_loop(0, n_tp, body, 0)

    conv_sem = recv_sem.at[jnp.where(t == n_tp - 1, 12, 0)]

    def send_conv(k, carry):
        p = lax.rem(t + k, n_tp)
        remote(dt_ref, steps.at[my_rows], send_sem.at[1], recv_sem.at[1], c, p).start()
        remote(conv_ref.at[:, columns(p, conv_width)], chan.at[my_rows], send_sem.at[0], conv_sem, c, p).start()
        return carry

    def send_gate(k, carry):
        p = lax.rem(t + k, n_tp)
        remote(
            gate_ref.at[:, columns(p, inner_width)], gates.at[my_rows], send_sem.at[4], recv_sem.at[4], c, p
        ).start()
        return carry

    send_heads(kv_ref, kv_width, raw_kv, 2)
    lax.fori_loop(1, n_tp, send_conv, 0)
    near(conv_ref.at[:, columns(t, conv_width)], chan.at[my_rows], conv_sem).start()
    near(dt_ref, steps.at[my_rows], recv_sem.at[1]).start()

    def region(buf, way, dist, parity, cut):
        slot = 2 * lax.rem(z - way * dist + nz, nz) + parity
        if not cut:
            return buf.at[slot]
        half = buf.shape[1] // 2
        return buf.at[slot, pl.ds(0 if way > 0 else half, half)]

    bufs = (kvc, kvp)

    def ring_copy(which, way, step, arriving):
        cut = step + 1 == far
        piece = region(bufs[which], way, step + 1 if arriving else step, core, cut)
        at = (which * 2 + (way < 0)) * far + step
        return remote(
            piece,
            piece,
            ring_send.at[at],
            ring_recv.at[at],
            2 * lax.rem(z + way + nz, nz) + yh,
            t,
        )

    def sib_copy(which, way, dist, arriving):
        cut = dist == far
        piece = region(bufs[which], way, dist, 1 - core if arriving else core, cut)
        at = (which * 2 + (way < 0)) * (far + 1) + dist
        return remote(piece, piece, sib_send.at[at], sib_recv.at[at], c, t + 1 - 2 * core)

    def ring_begin(which):
        for way in (1, -1):
            ring_copy(which, way, 0, False).start()
        sib_copy(which, 1, 0, False).start()

    def ring_advance(which, step):
        for way in (1, -1):
            ring_copy(which, way, step, True).wait_recv()
            if step + 1 < far:
                ring_copy(which, way, step + 1, False).start()
        for way in (1, -1):
            sib_copy(which, way, step + 1, False).start()

    def sib_wait(which, dist):
        for way in (1, -1) if dist else (1,):
            sib_copy(which, way, dist, True).wait_recv()

    wait_for(kvc.at[group], recv_sem.at[5])
    ring_begin(0)

    lane = lax.broadcasted_iota(jnp.int32, (rows, head), 1)
    sine = jnp.where(lane < head // 2, -sin_ref[...], sin_ref[...])
    cosine = cos_ref[...]

    def rotated(a):
        a = a.astype(F32)
        return (a * cosine + pltpu.roll(a, head // 2, 1) * sine).astype(BF16)

    wait_for(raw_kv, recv_sem.at[2])
    kvp[group] = jnp.concatenate([rotated(raw_kv[:, :head]), raw_kv[:, head:]], axis=1)
    ring_begin(1)

    first[...] = jnp.zeros(first.shape, F32)
    first[pl.ds(PAD - first_ref.shape[0], first_ref.shape[0]), :] = first_ref[...].astype(F32)
    n_heads = dt_bias_ref.shape[1]
    small_ref[...] = jnp.zeros(small_ref.shape, F32)
    small_ref[0:1, 0:n_heads] = dt_bias_ref[...]
    small_ref[1:2, 0:n_heads] = rate_ref[...]
    small_ref[2:3, 0:n_heads] = skip_ref[...]
    all_heads = steps.shape[1]
    pick = lax.broadcasted_iota(jnp.int32, (all_heads, 128), 0) == (
        t * n_heads + lax.broadcasted_iota(jnp.int32, (all_heads, 128), 1)
    )
    row_at = lax.broadcasted_iota(jnp.int32, (rows, rows), 0)
    col_at = lax.broadcasted_iota(jnp.int32, (rows, rows), 1)
    causal = row_at >= col_at
    wide_at = 2 * 128
    wait_for(steps, recv_sem.at[1])
    raw_step = fast_dot(steps[...], pick.astype(F32).astype(BF16)) + small_ref[0:1, :]
    step_size = jnp.maximum(raw_step, 0.0) + jnp.log1p(jnp.exp(-jnp.abs(raw_step)))
    log_decay = -jnp.exp(small_ref[1:2, :]) * step_size
    cumulative = exact_dot(causal.astype(F32), log_decay)
    cum_rows[...] = cumulative.T

    def spread_out(j, carry):
        cols = columns(j, wide_at)
        spread = lax.broadcasted_iota(jnp.int32, (128, wide_at), 0) == (
            j * (wide_at // phead) + lax.broadcasted_iota(jnp.int32, (128, wide_at), 1) // phead
        )
        spread = spread.astype(F32)
        cum_here = exact_dot(cumulative, spread)
        step_here = exact_dot(step_size, spread)
        cum_wide[:, cols] = cum_here
        grown[:, cols] = jnp.exp(cum_here)
        step_wide[:, cols] = step_here
        toward_wide[:, cols] = step_here * jnp.exp(cum_here[rows - 1 : rows] - cum_here)
        skip_wide[:, cols] = exact_dot(small_ref[...], spread)
        return carry

    lax.fori_loop(0, inner_width // wide_at, spread_out, 0)
    ring_advance(0, 0)

    last_rows = pl.ds(rows - PAD, PAD)
    wait_for(chan.at[last_rows], recv_sem.at[12])
    halo_copy = remote(
        chan.at[last_rows], halo, send_sem.at[6], recv_sem.at[6], lax.rem(c + 1, n_ctx), t
    )
    halo_copy.start()
    early_rows = pl.ds(0, rows - row_part)
    wait_for(chan.at[early_rows], recv_sem.at[0])
    send_heads(q_ref, q_width, raw_q, 3)
    halo_copy.wait_recv()
    n_taps = tap_ref.shape[0]
    piece = 256

    def convolve(j, carry):
        cols = columns(j, piece)
        before = jnp.where(c == 0, first[:, cols], halo[:, cols].astype(F32))
        wide = jnp.concatenate([before, chan[:, cols].astype(F32)], axis=0)
        total = bias_ref[cols][None, :]
        for tap in range(n_taps):
            start = PAD - (n_taps - 1) + tap
            total = total + tap_ref[pl.ds(tap, 1), cols] * wide[start : start + rows]
        mixed[:, cols] = silu(total)
        return carry

    lax.fori_loop(0, (inner_width + n_state) // piece, convolve, 0)
    ring_advance(1, 0)

    def states(k, carry):
        j = lax.rem(k + z // 2, inner_width // wide_at)
        cols = columns(j, wide_at)
        here = mixed[:, cols]
        high, low = halves(here * step_wide[:, cols])
        x_high[:, cols] = high
        x_low[:, cols] = low
        toward = here * toward_wide[:, cols]
        fresh = exact_dot(mixed[:, pl.ds(inner_width, n_state)], toward, (((0,), (0,)), ((), ())))
        fresh = fresh.astype(BF16)
        decay = grown[rows - 1 : rows, cols]
        decay_1 = decay.astype(BF16).astype(F32)
        decay_2 = (decay - decay_1).astype(BF16).astype(F32)
        decay_3 = decay - decay_1 - decay_2
        at = lax.broadcasted_iota(jnp.int32, (PAD, wide_at), 0)
        decays = jnp.where(at == 0, decay_1, jnp.where(at == 1, decay_2, jnp.where(at == 2, decay_3, 0.0)))
        decays = decays.astype(BF16)
        for k in range(2 * wide_at // 128):
            i = j * (2 * wide_at // 128) + k
            lanes = slice(k // 2 * 128, k // 2 * 128 + 128)
            start = k % 2 * half_state
            state_out[i, :half_state] = fresh[start : start + half_state, lanes]
            state_out[i, half_state:] = decays[:, lanes]

            @pl.when(i == c)
            def _(i=i):
                near(state_out.at[i], state_all.at[c], recv_sem.at[7]).start()

            @pl.when(i != c)
            def _(i=i):
                remote(state_out.at[i], state_all.at[c], send_sem.at[7], recv_sem.at[7], i, t).start()

        return carry

    lax.fori_loop(0, inner_width // wide_at, states, 0)

    ring_advance(0, 1)
    near(gate_ref.at[:, columns(t, inner_width)], gates.at[my_rows], recv_sem.at[4]).start()
    lax.fori_loop(1, n_tp, send_gate, 0)
    ring_advance(1, 1)
    lax.fori_loop((inner_width + n_state) // piece, conv_width // piece, convolve, 0)

    contact[...] = exact_dot(
        mixed[:, pl.ds(inner_width + n_state, n_state)],
        mixed[:, pl.ds(inner_width, n_state)],
        (((1,), (1,)), ((), ())),
    )
    pair_lane = lax.broadcasted_iota(jnp.int32, (rows, 128), 1)

    def within(j, carry):
        cols = columns(j, 128)
        cum_pair = cum_wide[:, cols]
        both = jnp.concatenate([x_high[:, cols], x_low[:, cols]], axis=1)
        parts = []
        for k in range(2):
            gap = cum_pair[:, k * phead : k * phead + 1] - cum_rows[pl.ds(2 * j + k, 1), :]
            mixing = contact[...] * jnp.exp(jnp.where(causal, gap, HIDDEN))
            high, low = halves(mixing)
            product = fast_dot(high, both)
            parts.append(product[:, :128] + product[:, 128:] + fast_dot(low, both[:, :128]))
        inner[:, cols] = mixed[:, cols] * skip_wide[2:3, cols] + jnp.where(
            pair_lane < phead, parts[0], parts[1]
        )
        return carry

    lax.fori_loop(0, inner_width // 128, within, 0)
    ring_advance(0, 2)

    wait_for(raw_q, recv_sem.at[3])
    mark = (lax.broadcasted_iota(jnp.int32, (rows, head), 1) == 0).astype(F32).astype(BF16)
    for h in range(local_q):
        part = rotated(raw_q[:, h * head : (h + 1) * head])
        queries[pl.ds(h * rows, rows), :] = jnp.concatenate([part, mark], axis=1)
    top[...] = jnp.full(top.shape, FLOOR, F32)
    acc[...] = jnp.zeros(acc.shape, F32)
    factor = math.log2(math.e) / math.sqrt(head)
    length = length_ref[0]
    pair_rows = 2 * cache_rows

    def update(key, value, diagonal):
        for h in range(local_q):
            at = pl.ds(h * rows, rows)
            score = fast_dot(queries[at, :], key, (((1,), (1,)), ((), ())))
            if diagonal:
                shape = (rows, 2 * rows)
                seen = lax.broadcasted_iota(jnp.int32, shape, 1) <= (
                    core * rows + lax.broadcasted_iota(jnp.int32, shape, 0)
                )
                masked = jnp.where(seen, score[:, pair_rows:], HIDDEN)
                score = jnp.concatenate([score[:, :pair_rows], masked], axis=1)
            old = top[at, :]
            new = jnp.maximum(old, jnp.max(score, axis=1, keepdims=True))
            top[at, :] = new
            weight = jnp.exp2((score - widened(new, score.shape[1])) * factor)
            scale = jnp.exp2((old - new) * factor)
            acc[at, :] = acc[at, :] * widened(scale, 2 * head) + fast_dot(weight.astype(BF16), value)

    def attend(place):
        def run(prompt, diagonal):
            lanes = lax.broadcasted_iota(jnp.int32, (pair_rows, head), 1)
            slots = place * pair_rows + lax.broadcasted_iota(jnp.int32, (pair_rows, head), 0)
            hide = jnp.where(jnp.logical_and(lanes == 0, slots >= length), HIDDEN, 0.0).astype(BF16)
            block = kvc[pl.ds(2 * place, 2)].reshape(pair_rows, 2 * head)
            key, value = block[:, :head], block[:, head:]
            if prompt:
                more = kvp[pl.ds(2 * place, 2)].reshape(2 * rows, 2 * head)
                key = jnp.concatenate([key, more[:, :head]], axis=0)
                value = jnp.concatenate([value, more[:, head:]], axis=0)
                hide = jnp.concatenate([hide, jnp.zeros((2 * rows, head), BF16)], axis=0)
            ones = jnp.ones(value.shape, BF16)
            update(
                jnp.concatenate([key, hide], axis=1), jnp.concatenate([value, ones], axis=1), diagonal
            )

        pl.when(place < z)(functools.partial(run, True, False))
        pl.when(place == z)(functools.partial(run, True, True))
        pl.when(place > z)(functools.partial(run, False, False))

    def pass_states():
        wait_for(state_all, recv_sem.at[7])
        init_copy.wait()

        def scan_group(i, state):
            enter_out[i] = state.astype(BF16)
            parts = state_all[i, half_state:].astype(F32)
            decay = parts[0:1] + parts[1:2] + parts[2:3]
            return decay * state + state_all[i, :half_state].astype(F32)

        lax.fori_loop(0, n_ctx, scan_group, init_piece[...].reshape(128, half_state).T)

        def send_enter(k, carry):
            i = lax.rem(c + k, n_ctx)
            remote(
                enter_out.at[i], enter_all.at[own_rows, own_cols], send_sem.at[9], recv_sem.at[9], i, t
            ).start()
            return carry

        near(enter_out.at[c], enter_all.at[own_rows, own_cols], recv_sem.at[9]).start()
        lax.fori_loop(1, n_ctx, send_enter, 0)

    def attend_next(k, carry):
        @pl.when(k == 0)
        def _():
            for dist in range(2):
                sib_wait(0, dist)
                sib_wait(1, dist)

        @pl.when(k == 1)
        def _():
            ring_advance(1, 2)

        @pl.when(k == 2)
        def _():
            ring_advance(0, 3)

        @pl.when(k == 3)
        def _():
            ring_advance(1, 3)
            pass_states()
            for dist in range(2, far + 1):
                sib_wait(0, dist)
                sib_wait(1, dist)

        back = lax.rem(k, 2) == 0
        attend(lax.rem(jnp.where(back, z + nz - k // 2, z + (k + 1) // 2), nz))
        return carry

    lax.fori_loop(0, nz, attend_next, 0)
    for h in range(local_q):
        found = acc[pl.ds(h * rows, rows), :]
        attn_loc[:, h * head : (h + 1) * head] = (found[:, :head] / found[:, head:]).astype(BF16)

    def send_attn(p, carry):
        src = attn_loc.at[pl.ds(pl.multiple_of(p * row_part, 16), row_part)]
        dst = attn_ref.at[:, columns(t - core + yh, q_width)]
        own = jnp.logical_and(group == c, p == t)

        @pl.when(own)
        def _():
            near(src, dst, recv_sem.at[10]).start()

        @pl.when(jnp.logical_not(own))
        def _():
            remote(src, dst, send_sem.at[10], recv_sem.at[10], group, p).start()

        return carry

    lax.fori_loop(0, n_tp, send_attn, 0)

    wait_for(enter_all, recv_sem.at[9])
    wait_for(gates, recv_sem.at[4])
    per_block = min(4, n_tp)
    block = per_block * row_part
    parts = rows // block

    def finish(k, carry):
        part = lax.rem(k + t // per_block, parts)
        at = pl.ds(pl.multiple_of(part * block, 16), block)
        out_high, out_low = halves(mixed[at, pl.ds(inner_width + n_state, n_state)])
        carried = fast_dot(out_high, enter_all[...]) + fast_dot(out_low, enter_all[...])
        y = inner[at, :] + grown[at, :] * carried
        gated = y * silu(gates[at, :].astype(F32))
        square = jnp.sum(gated * gated, axis=1, keepdims=True)
        norm = lax.rsqrt(square / inner_width + 1e-05)
        mamba_loc[at, :] = (gated * norm * gain_ref[...]).astype(BF16)
        for i in range(per_block):
            p = part * per_block + i
            src = mamba_loc.at[pl.ds(pl.multiple_of(p * row_part, 16), row_part)]
            dst = mamba_ref.at[:, columns(t, inner_width)]

            @pl.when(p == t)
            def _(src=src, dst=dst):
                near(src, dst, recv_sem.at[11]).start()

            @pl.when(p != t)
            def _(src=src, dst=dst, p=p):
                remote(src, dst, send_sem.at[11], recv_sem.at[11], c, p).start()

        return carry

    lax.fori_loop(0, parts, finish, 0)

    wait_for(attn_ref, recv_sem.at[10])
    wait_for(mamba_ref, recv_sem.at[11])
    others = (n_tp - 1) * row_part
    wait_for(chan.at[pl.ds(0, others)], send_sem.at[0])
    wait_for(steps.at[pl.ds(0, others)], send_sem.at[1])
    wait_for(gates.at[pl.ds(0, others)], send_sem.at[4])
    wait_for(mamba_loc.at[pl.ds(0, others)], send_sem.at[11])
    for ref, which in ((raw_kv, 2), (raw_q, 3), (attn_loc, 10)):

        @pl.when(on_diagonal)
        def _(ref=ref, which=which):
            wait_for(ref.at[pl.ds(0, others)], send_sem.at[which])

        @pl.when(jnp.logical_not(on_diagonal))
        def _(ref=ref, which=which):
            wait_for(ref, send_sem.at[which])

    @pl.when(jnp.logical_not(on_diagonal))
    def _():
        wait_for(cache_ref, send_sem.at[5])

    halo_copy.wait_send()
    wait_for(state_all.at[pl.ds(0, n_ctx - 1)], send_sem.at[7])
    wait_for(enter_out.at[pl.ds(0, n_ctx - 1)], send_sem.at[9])
    for which in range(2):
        for way in (1, -1):
            for step in range(far):
                ring_copy(which, way, step, False).wait_send()
        sib_copy(which, 1, 0, False).wait_send()
        for dist in range(1, far + 1):
            for way in (1, -1):
                sib_copy(which, way, dist, False).wait_send()


def group_of_partner(z, yh):
    return 2 * z + yh


def local(
    queries,
    keyvals,
    cache_kv,
    conv_input,
    gate_input,
    dt_raw,
    conv_weight,
    conv_bias,
    dt_bias,
    decay_log,
    skip_weight,
    norm_gain,
    ssm_init,
    conv_init,
    prompt_start,
    cache_length,
):
    n_ctx = lax.axis_size("ctx")
    n_tp = lax.axis_size("tp")
    c = lax.axis_index("ctx")
    t = lax.axis_index("tp")
    head = cache_kv.shape[1] // 2
    row_part = queries.shape[0]
    rows = row_part * n_tp
    n_heads, phead, n_state = ssm_init.shape
    inner_width = n_heads * phead
    conv_width = conv_weight.shape[1]
    q_width = queries.shape[1] // n_tp
    cache_rows = cache_kv.shape[0]
    far = n_ctx // 4

    group = (c // 2) * 2 + t % 2
    half_width = head // 2
    lane_index = (jnp.arange(head, dtype=jnp.int32) % half_width).astype(F32)
    inverse = jnp.power(F32(10000.0), -lane_index / half_width)
    positions = prompt_start[0] + group * rows + jnp.arange(rows, dtype=jnp.int32)
    angles = positions.astype(F32)[:, None] * inverse[None, :]
    hbm = pl.BlockSpec(memory_space=pl.ANY)
    vmem = pl.BlockSpec(memory_space=pltpu.VMEM)
    smem = pl.BlockSpec(memory_space=pltpu.SMEM)
    dma = pltpu.SemaphoreType.DMA
    local_rows = rows * q_width // head
    return pl.pallas_call(
        functools.partial(kernel, n_ctx, n_tp, phead),
        out_shape=(
            jax.ShapeDtypeStruct(queries.shape, BF16),
            jax.ShapeDtypeStruct(gate_input.shape, BF16),
        ),
        in_specs=[smem] + [hbm] * 7 + [vmem] * 9,
        out_specs=(hbm, hbm),
        scratch_shapes=[
            pltpu.VMEM((n_ctx, cache_rows, 2 * head), BF16),
            pltpu.VMEM((n_ctx, rows, 2 * head), BF16),
            pltpu.VMEM((rows, 2 * head), BF16),
            pltpu.VMEM((rows, q_width), BF16),
            pltpu.VMEM((rows, conv_width), BF16),
            pltpu.VMEM((PAD, conv_width), BF16),
            pltpu.VMEM((rows, inner_width), BF16),
            pltpu.VMEM((rows, dt_raw.shape[1]), BF16),
            pltpu.VMEM((rows, conv_width), F32),
            pltpu.VMEM((rows, inner_width), BF16),
            pltpu.VMEM((rows, inner_width), BF16),
            pltpu.VMEM((rows, inner_width), F32),
            pltpu.VMEM((rows, inner_width), F32),
            pltpu.VMEM((rows, inner_width), F32),
            pltpu.VMEM((rows, inner_width), F32),
            pltpu.VMEM((rows, inner_width), F32),
            pltpu.VMEM((8, inner_width), F32),
            pltpu.VMEM((128, rows), F32),
            pltpu.VMEM((rows, rows), F32),
            pltpu.VMEM((n_ctx, n_state // 2 + PAD, 128), BF16),
            pltpu.VMEM((n_ctx, n_state // 2 + PAD, 128), BF16),
            pltpu.VMEM((n_ctx, n_state // 2, 128), BF16),
            pltpu.VMEM((n_state, inner_width), BF16),
            pltpu.VMEM((local_rows, 2 * head), BF16),
            pltpu.VMEM((local_rows, 128), F32),
            pltpu.VMEM((local_rows, 2 * head), F32),
            pltpu.VMEM((rows, q_width), BF16),
            pltpu.VMEM((rows, inner_width), BF16),
            pltpu.VMEM((PAD, conv_width), F32),
            pltpu.VMEM((8, 128), F32),
            pltpu.VMEM((128 // phead, phead, n_state // 2), F32),
            dma((12,)),
            dma((13,)),
            dma((4 * far,)),
            dma((4 * far,)),
            dma((4 * (far + 1),)),
            dma((4 * (far + 1),)),
        ],
        compiler_params=pltpu.CompilerParams(
            collective_id=0, has_side_effects=True, vmem_limit_bytes=62 * 1024 * 1024
        ),
        cost_estimate=pl.CostEstimate(
            flops=8 * 10**9, bytes_accessed=6 * 10**6, transcendentals=14 * 10**6
        ),
    )(
        cache_length,
        queries,
        keyvals,
        cache_kv,
        conv_input,
        gate_input,
        dt_raw,
        ssm_init,
        conv_init,
        conv_weight,
        conv_bias,
        dt_bias[None, :],
        decay_log[None, :],
        skip_weight[None, :],
        norm_gain[None, :],
        jnp.cos(angles),
        jnp.sin(angles),
    )


def solution(mesh):
    return jax.shard_map(
        local,
        mesh=mesh,
        in_specs=(
            P(("ctx", "tp"), None),
            P(("ctx", "tp"), None),
            P("ctx", "tp"),
            P(("ctx", "tp"), None),
            P(("ctx", "tp"), None),
            P(("ctx", "tp"), None),
            P(None, "tp"),
            P("tp"),
            P("tp"),
            P("tp"),
            P("tp"),
            P("tp"),
            P("tp", None, None),
            P(None, "tp"),
            P(),
            P(),
        ),
        out_specs=(P(("ctx", "tp"), None), P(("ctx", "tp"), None)),
        check_vma=False,
    )
```

```python
import functools
import math

import jax
import jax.numpy as jnp
from jax import lax
from jax.experimental import pallas as pl
from jax.experimental.pallas import tpu as pltpu
from jax.sharding import PartitionSpec as P

HIGHEST = lax.Precision.HIGHEST
F32 = jnp.float32
BF16 = jnp.bfloat16
MESH = pl.DeviceIdType.MESH
PAD = 16
FLOOR = -1e20
HIDDEN = -1e30


def exact_dot(a, b, dims=(((1,), (0,)), ((), ()))):
    return lax.dot_general(a, b, dims, precision=HIGHEST, preferred_element_type=F32)


def fast_dot(a, b, dims=(((1,), (0,)), ((), ()))):
    return lax.dot_general(a, b, dims, preferred_element_type=F32)


def halves(a):
    high = a.astype(BF16)
    return high, (a - high.astype(F32)).astype(BF16)


def silu(a):
    return a / (1.0 + jnp.exp(-a))


def widened(a, width):
    return jnp.tile(a, (1, -(-width // a.shape[1])))[:, :width]


def kernel(
    n_ctx,
    n_tp,
    phead,
    length_ref,
    q_ref,
    kv_ref,
    cache_ref,
    conv_ref,
    gate_ref,
    dt_ref,
    init_ref,
    first_ref,
    tap_ref,
    bias_ref,
    dt_bias_ref,
    rate_ref,
    skip_ref,
    gain_ref,
    cos_ref,
    sin_ref,
    attn_ref,
    mamba_ref,
    kvc,
    kvp,
    raw_kv,
    raw_q,
    chan,
    halo,
    gates,
    steps,
    mixed,
    x_high,
    x_low,
    inner,
    grown,
    cum_wide,
    step_wide,
    toward_wide,
    skip_wide,
    cum_rows,
    contact,
    state_out,
    state_all,
    enter_out,
    enter_all,
    queries,
    top,
    acc,
    attn_loc,
    mamba_loc,
    first,
    small_ref,
    init_piece,
    middle,
    next_high,
    next_low,
    squares,
    square_out,
    square_in,
    send_sem,
    recv_sem,
    ring_send,
    ring_recv,
    sib_send,
    sib_recv,
):
    c = lax.axis_index("ctx")
    t = lax.axis_index("tp")
    nz = n_ctx // 2
    far = nz // 2
    z = c // 2
    yh = lax.rem(c, 2)
    core = lax.rem(t, 2)
    group = 2 * z + core
    row_part = q_ref.shape[0]
    rows = row_part * n_tp
    q_width = raw_q.shape[1]
    kv_width = raw_kv.shape[1]
    head = kv_width // 2
    local_q = q_width // head
    conv_width = tap_ref.shape[1]
    inner_width = gain_ref.shape[1]
    n_state = (conv_width - inner_width) // 2
    half_width = gates.shape[1]
    own_width = chan.shape[1]
    both_rows = 2 * rows
    cache_rows = kvc.shape[1]
    my_rows = pl.ds(pl.multiple_of(t * row_part, 16), row_part)
    on_diagonal = yh == core
    plane_rows = pl.ds(pl.multiple_of(yh * rows + t * row_part, 16), row_part)

    def columns(index, width):
        return pl.ds(pl.multiple_of(index * width, 128), width)

    def remote(src, dst, s_sem, r_sem, ctx_id, tp_id):
        return pltpu.make_async_remote_copy(
            src_ref=src,
            dst_ref=dst,
            send_sem=s_sem,
            recv_sem=r_sem,
            device_id=(ctx_id, tp_id),
            device_id_type=MESH,
        )

    def near(src, dst, sem):
        return pltpu.make_async_copy(src, dst, sem)

    def wait_for(ref, sem):
        near(ref, ref, sem).wait()

    barrier = pltpu.get_barrier_semaphore()

    def greet(ctx_id, tp_id):
        pl.semaphore_signal(barrier, inc=1, device_id=(ctx_id, tp_id), device_id_type=MESH)

    def greet_plane(k, carry):
        greet(2 * z + 1 - yh, k)

        @pl.when(k > 0)
        def _():
            greet(c, lax.rem(t + k, n_tp))

        return carry

    lax.fori_loop(0, n_tp, greet_plane, 0)

    def greet_line(k, carry):
        greet(2 * lax.rem(z + k, nz) + yh, t)
        return carry

    lax.fori_loop(1, nz, greet_line, 0)
    pl.semaphore_wait(barrier, 2 * n_tp - 1 + nz - 1)

    half_state = n_state // 2
    own_rows = pl.ds(pl.multiple_of(lax.rem(z, 2) * half_state, 128), half_state)
    own_cols = columns(z // 2, 128)
    pair = 128 // phead
    n_heads = dt_bias_ref.shape[1]
    init_copy = near(
        init_ref.at[pl.ds(yh * (n_heads // 2) + (z // 2) * pair, pair), :, own_rows],
        init_piece,
        recv_sem.at[8],
    )
    init_copy.start()

    @pl.when(on_diagonal)
    def _():
        near(cache_ref, kvc.at[group], recv_sem.at[5]).start()

    @pl.when(jnp.logical_not(on_diagonal))
    def _():
        remote(
            cache_ref, kvc.at[group_of_partner(z, yh)], send_sem.at[5], recv_sem.at[5], group, t - core + yh
        ).start()

    def send_heads(src_ref, width, dst_ref, which):
        def body(k, carry):
            h = lax.rem(t + k, n_tp)
            to_ctx = 2 * z + lax.rem(h, 2)
            to_tp = (h // 2) * 2 + yh
            own = jnp.logical_and(to_ctx == c, to_tp == t)
            src = src_ref.at[:, columns(h, width)]
            dst = dst_ref.at[my_rows]

            @pl.when(own)
            def _():
                near(src, dst, recv_sem.at[which]).start()

            @pl.when(jnp.logical_not(own))
            def _():
                remote(src, dst, send_sem.at[which], recv_sem.at[which], to_ctx, to_tp).start()

            return carry

        lax.fori_loop(0, n_tp, body, 0)

    is_last = jnp.logical_and(t == n_tp - 1, yh == 1)
    conv_sem = recv_sem.at[jnp.where(is_last, 12, 0)]
    dt_width = steps.shape[1]
    per_dt = dt_width // n_heads

    def mixer_pieces(half, p):
        begin = p * conv_width
        return (
            (dt_ref.at[:, columns(p // per_dt, dt_width)], steps.at[plane_rows], 1),
            (
                conv_ref.at[:, pl.ds(pl.multiple_of(begin + half * half_width, 128), half_width)],
                chan.at[plane_rows, pl.ds(0, half_width)],
                0,
            ),
            (
                conv_ref.at[:, pl.ds(pl.multiple_of(begin + inner_width, 128), 2 * n_state)],
                chan.at[plane_rows, pl.ds(half_width, 2 * n_state)],
                0,
            ),
        )

    def gate_piece(half, p):
        return gate_ref.at[:, pl.ds(pl.multiple_of(p * inner_width + half * half_width, 128), half_width)]

    def plane_peer(k):
        return lax.rem(yh + k // n_tp, 2), lax.rem(t + k, n_tp)

    def send_mixer(k, carry):
        half, p = plane_peer(k)
        for src, dst, which in mixer_pieces(half, p):
            to_sem = recv_sem.at[which] if which else conv_sem
            remote(src, dst, send_sem.at[which], to_sem, 2 * z + half, p).start()
        return carry

    def send_gate(k, carry):
        half, p = plane_peer(k)
        remote(
            gate_piece(half, p), gates.at[plane_rows], send_sem.at[4], recv_sem.at[4], 2 * z + half, p
        ).start()
        return carry

    send_heads(kv_ref, kv_width, raw_kv, 2)
    lax.fori_loop(1, 2 * n_tp, send_mixer, 0)
    for src, dst, which in mixer_pieces(yh, t):
        near(src, dst, recv_sem.at[which] if which else conv_sem).start()

    def region(buf, way, dist, parity, cut):
        slot = 2 * lax.rem(z - way * dist + nz, nz) + parity
        if not cut:
            return buf.at[slot]
        half = buf.shape[1] // 2
        return buf.at[slot, pl.ds(0 if way > 0 else half, half)]

    bufs = (kvc, kvp)

    def ring_copy(which, way, step, arriving):
        cut = step + 1 == far
        piece = region(bufs[which], way, step + 1 if arriving else step, core, cut)
        at = (which * 2 + (way < 0)) * far + step
        return remote(
            piece,
            piece,
            ring_send.at[at],
            ring_recv.at[at],
            2 * lax.rem(z + way + nz, nz) + yh,
            t,
        )

    def sib_copy(which, way, dist, arriving):
        cut = dist == far
        piece = region(bufs[which], way, dist, 1 - core if arriving else core, cut)
        at = (which * 2 + (way < 0)) * (far + 1) + dist
        return remote(piece, piece, sib_send.at[at], sib_recv.at[at], c, t + 1 - 2 * core)

    def ring_begin(which):
        for way in (1, -1):
            ring_copy(which, way, 0, False).start()
        sib_copy(which, 1, 0, False).start()

    def ring_advance(which, step):
        for way in (1, -1):
            ring_copy(which, way, step, True).wait_recv()
            if step + 1 < far:
                ring_copy(which, way, step + 1, False).start()
        for way in (1, -1):
            sib_copy(which, way, step + 1, False).start()

    def sib_wait(which, dist):
        for way in (1, -1) if dist else (1,):
            sib_copy(which, way, dist, True).wait_recv()

    wait_for(kvc.at[group], recv_sem.at[5])
    ring_begin(0)

    lane = lax.broadcasted_iota(jnp.int32, (rows, head), 1)
    sine = jnp.where(lane < head // 2, -sin_ref[...], sin_ref[...])
    cosine = cos_ref[...]

    def rotated(a):
        a = a.astype(F32)
        return (a * cosine + pltpu.roll(a, head // 2, 1) * sine).astype(BF16)

    wait_for(raw_kv, recv_sem.at[2])
    kvp[group] = jnp.concatenate([rotated(raw_kv[:, :head]), raw_kv[:, head:]], axis=1)
    ring_begin(1)

    first[...] = jnp.zeros(first.shape, F32)
    first[pl.ds(PAD - first_ref.shape[0], first_ref.shape[0]), :] = first_ref[...].astype(F32)
    small_ref[...] = jnp.zeros(small_ref.shape, F32)
    small_ref[0:1, 0:n_heads] = dt_bias_ref[...]
    small_ref[1:2, 0:n_heads] = rate_ref[...]
    small_ref[2:3, 0:n_heads] = skip_ref[...]
    half_heads = n_heads // 2
    to_lane = lax.broadcasted_iota(jnp.int32, (128, 128), 1)
    of_half = jnp.logical_and(
        lax.broadcasted_iota(jnp.int32, (128, 128), 0) == yh * half_heads + to_lane, to_lane < half_heads
    )
    small = exact_dot(small_ref[...], of_half.astype(F32))
    pick = lax.broadcasted_iota(jnp.int32, (dt_width, 128), 0) == (
        lax.rem(t, per_dt) * n_heads
        + yh * half_heads
        + lax.broadcasted_iota(jnp.int32, (dt_width, 128), 1)
    )
    row_at = lax.broadcasted_iota(jnp.int32, (rows, rows), 0)
    col_at = lax.broadcasted_iota(jnp.int32, (rows, rows), 1)
    causal = row_at >= col_at
    wide_at = 2 * 128
    wait_for(steps, recv_sem.at[1])
    raw_step = fast_dot(steps[...], pick.astype(F32).astype(BF16)) + small[0:1]
    step_size = jnp.maximum(raw_step, 0.0) + jnp.log1p(jnp.exp(-jnp.abs(raw_step)))
    log_decay = -jnp.exp(small[1:2]) * step_size
    tri = causal.astype(F32)
    cumulative = jnp.concatenate(
        [exact_dot(tri, log_decay[:rows]), exact_dot(tri, log_decay[rows:])], axis=0
    )
    cum_rows[...] = cumulative.T

    def spread_out(j, carry):
        cols = columns(j, wide_at)
        spread = lax.broadcasted_iota(jnp.int32, (128, wide_at), 0) == (
            j * (wide_at // phead) + lax.broadcasted_iota(jnp.int32, (128, wide_at), 1) // phead
        )
        spread = spread.astype(F32)
        for part in range(2):
            at = pl.ds(part * rows, rows)
            here = slice(part * rows, part * rows + rows)
            cum_here = exact_dot(cumulative[here], spread)
            step_here = exact_dot(step_size[here], spread)
            cum_wide[at, cols] = cum_here
            grown[at, cols] = jnp.exp(cum_here)
            step_wide[at, cols] = step_here
            toward_wide[at, cols] = step_here * jnp.exp(cum_here[rows - 1 : rows] - cum_here)
        skip_wide[:, cols] = exact_dot(small, spread)
        return carry

    lax.fori_loop(0, half_width // wide_at, spread_out, 0)
    ring_advance(0, 0)
    ring_advance(1, 0)

    last_rows = pl.ds(both_rows - PAD, PAD)
    wait_for(chan.at[last_rows], recv_sem.at[12])
    halo_copy = remote(
        chan.at[last_rows], halo, send_sem.at[6], recv_sem.at[6], 2 * lax.rem(z + 1, nz) + yh, t
    )
    halo_copy.start()
    wait_for(chan.at[pl.ds(0, both_rows - row_part)], recv_sem.at[0])
    send_heads(q_ref, q_width, raw_q, 3)
    halo_copy.wait_recv()
    n_taps = tap_ref.shape[0]
    piece = 256

    def convolve(j, carry):
        cols = columns(j, piece)
        begin = j * piece + jnp.where(j * piece < half_width, yh * half_width, inner_width - half_width)
        from_cols = pl.ds(pl.multiple_of(begin, 128), piece)
        before = jnp.where(z == 0, first[:, from_cols], halo[:, cols].astype(F32))
        wide = jnp.concatenate([before, chan[:, cols].astype(F32)], axis=0)
        total = bias_ref[from_cols][None, :]
        for tap in range(n_taps):
            start = PAD - (n_taps - 1) + tap
            total = total + tap_ref[pl.ds(tap, 1), from_cols] * wide[start : start + both_rows]
        mixed[:, cols] = silu(total)
        return carry

    lax.fori_loop(0, (half_width + n_state) // piece, convolve, 0)
    in_cols = pl.ds(half_width, n_state)
    out_cols = pl.ds(half_width + n_state, n_state)

    def states(k, carry):
        @pl.when(k == 1)
        def _():
            ring_advance(0, 1)

        j = lax.rem(k + z // far, half_width // wide_at)
        cols = columns(j, wide_at)
        fresh = []
        for part in range(2):
            at = pl.ds(part * rows, rows)
            here = mixed[at, cols]
            high, low = halves(here * step_wide[at, cols])
            x_high[at, cols] = high
            x_low[at, cols] = low
            toward = here * toward_wide[at, cols]
            fresh.append(exact_dot(mixed[at, in_cols], toward, (((0,), (0,)), ((), ()))))
        middle[:, cols] = fresh[0]
        later = grown[both_rows - 1 : both_rows, cols]
        fresh = later * fresh[0] + fresh[1]
        fresh = fresh.astype(BF16)
        decay = grown[rows - 1 : rows, cols] * later
        decay_1 = decay.astype(BF16).astype(F32)
        decay_2 = (decay - decay_1).astype(BF16).astype(F32)
        decay_3 = decay - decay_1 - decay_2
        at = lax.broadcasted_iota(jnp.int32, (PAD, wide_at), 0)
        decays = jnp.where(at == 0, decay_1, jnp.where(at == 1, decay_2, jnp.where(at == 2, decay_3, 0.0)))
        decays = decays.astype(BF16)
        for k in range(2 * wide_at // 128):
            i = j * (2 * wide_at // 128) + k
            lanes = slice(k // 2 * 128, k // 2 * 128 + 128)
            start = k % 2 * half_state
            state_out[i, :half_state] = fresh[start : start + half_state, lanes]
            state_out[i, half_state:] = decays[:, lanes]

            @pl.when(i == z)
            def _(i=i):
                near(state_out.at[i], state_all.at[z], recv_sem.at[7]).start()

            @pl.when(i != z)
            def _(i=i):
                remote(
                    state_out.at[i], state_all.at[z], send_sem.at[7], recv_sem.at[7], 2 * i + yh, t
                ).start()

        return carry

    lax.fori_loop(0, half_width // wide_at, states, 0)
    near(gate_piece(yh, t), gates.at[plane_rows], recv_sem.at[4]).start()
    lax.fori_loop(1, 2 * n_tp, send_gate, 0)
    ring_advance(1, 1)
    lax.fori_loop((half_width + n_state) // piece, own_width // piece, convolve, 0)

    for part in range(2):
        at = pl.ds(part * rows, rows)
        contact[part] = exact_dot(mixed[at, out_cols], mixed[at, in_cols], (((1,), (1,)), ((), ())))
    pair_lane = lax.broadcasted_iota(jnp.int32, (rows, 128), 1)
    pairs = half_width // 128

    def within(k, carry):
        @pl.when(k == pairs)
        def _():
            ring_advance(0, 2)

        part = k // pairs
        j = lax.rem(k, pairs)
        at = pl.ds(pl.multiple_of(part * rows, 16), rows)
        cols = columns(j, 128)
        cum_pair = cum_wide[at, cols]
        both = jnp.concatenate([x_high[at, cols], x_low[at, cols]], axis=1)
        pieces = []
        for i in range(2):
            row = cum_rows[pl.ds(2 * j + i, 1), :]
            row = jnp.where(part == 0, row[:, :rows], row[:, rows:])
            gap = cum_pair[:, i * phead : i * phead + 1] - row
            mixing = contact[part] * jnp.exp(jnp.where(causal, gap, HIDDEN))
            high, low = halves(mixing)
            product = fast_dot(high, both)
            pieces.append(product[:, :128] + product[:, 128:] + fast_dot(low, both[:, :128]))
        inner[at, cols] = mixed[at, cols] * skip_wide[2:3, cols] + jnp.where(
            pair_lane < phead, pieces[0], pieces[1]
        )
        return carry

    lax.fori_loop(0, 2 * pairs, within, 0)
    ring_advance(1, 2)

    wait_for(raw_q, recv_sem.at[3])
    mark = (lax.broadcasted_iota(jnp.int32, (rows, head), 1) == 0).astype(F32).astype(BF16)
    for h in range(local_q):
        part = rotated(raw_q[:, h * head : (h + 1) * head])
        queries[pl.ds(h * rows, rows), :] = jnp.concatenate([part, mark], axis=1)
    top[...] = jnp.full(top.shape, FLOOR, F32)
    acc[...] = jnp.zeros(acc.shape, F32)
    factor = math.log2(math.e) / math.sqrt(head)
    length = length_ref[0]
    pair_rows = 2 * cache_rows

    def update(key, value, diagonal):
        for h in range(local_q):
            at = pl.ds(h * rows, rows)
            score = fast_dot(queries[at, :], key, (((1,), (1,)), ((), ())))
            if diagonal:
                shape = (rows, 2 * rows)
                seen = lax.broadcasted_iota(jnp.int32, shape, 1) <= (
                    core * rows + lax.broadcasted_iota(jnp.int32, shape, 0)
                )
                masked = jnp.where(seen, score[:, pair_rows:], HIDDEN)
                score = jnp.concatenate([score[:, :pair_rows], masked], axis=1)
            old = top[at, :]
            new = jnp.maximum(old, jnp.max(score, axis=1, keepdims=True))
            top[at, :] = new
            weight = jnp.exp2((score - widened(new, score.shape[1])) * factor)
            scale = jnp.exp2((old - new) * factor)
            acc[at, :] = acc[at, :] * widened(scale, 2 * head) + fast_dot(weight.astype(BF16), value)

    def attend(place):
        def run(prompt, diagonal):
            lanes = lax.broadcasted_iota(jnp.int32, (pair_rows, head), 1)
            slots = place * pair_rows + lax.broadcasted_iota(jnp.int32, (pair_rows, head), 0)
            hide = jnp.where(jnp.logical_and(lanes == 0, slots >= length), HIDDEN, 0.0).astype(BF16)
            block = kvc[pl.ds(2 * place, 2)].reshape(pair_rows, 2 * head)
            key, value = block[:, :head], block[:, head:]
            if prompt:
                more = kvp[pl.ds(2 * place, 2)].reshape(2 * rows, 2 * head)
                key = jnp.concatenate([key, more[:, :head]], axis=0)
                value = jnp.concatenate([value, more[:, head:]], axis=0)
                hide = jnp.concatenate([hide, jnp.zeros((2 * rows, head), BF16)], axis=0)
            ones = jnp.ones(value.shape, BF16)
            update(
                jnp.concatenate([key, hide], axis=1), jnp.concatenate([value, ones], axis=1), diagonal
            )

        pl.when(place < z)(functools.partial(run, True, False))
        pl.when(place == z)(functools.partial(run, True, True))
        pl.when(place > z)(functools.partial(run, False, False))

    def pass_states():
        wait_for(state_all, recv_sem.at[7])
        init_copy.wait()

        def scan_group(i, state):
            enter_out[i] = state.astype(BF16)
            parts = state_all[i, half_state:].astype(F32)
            decay = parts[0:1] + parts[1:2] + parts[2:3]
            return decay * state + state_all[i, :half_state].astype(F32)

        lax.fori_loop(0, nz, scan_group, init_piece[...].reshape(128, half_state).T)

        def send_enter(k, carry):
            i = lax.rem(z + k, nz)
            remote(
                enter_out.at[i],
                enter_all.at[own_rows, own_cols],
                send_sem.at[9],
                recv_sem.at[9],
                2 * i + yh,
                t,
            ).start()
            return carry

        near(enter_out.at[z], enter_all.at[own_rows, own_cols], recv_sem.at[9]).start()
        lax.fori_loop(1, nz, send_enter, 0)

    def attend_next(k, carry):
        @pl.when(k == 0)
        def _():
            for dist in range(2):
                sib_wait(0, dist)
                sib_wait(1, dist)

        @pl.when(k == 2)
        def _():
            ring_advance(0, 3)

        @pl.when(k == 3)
        def _():
            ring_advance(1, 3)
            pass_states()
            for dist in range(2, far + 1):
                sib_wait(0, dist)
                sib_wait(1, dist)

        back = lax.rem(k, 2) == 0
        attend(lax.rem(jnp.where(back, z + nz - k // 2, z + (k + 1) // 2), nz))
        return carry

    lax.fori_loop(0, nz, attend_next, 0)
    for h in range(local_q):
        found = acc[pl.ds(h * rows, rows), :]
        attn_loc[:, h * head : (h + 1) * head] = (found[:, :head] / found[:, head:]).astype(BF16)

    def send_attn(p, carry):
        src = attn_loc.at[pl.ds(pl.multiple_of(p * row_part, 16), row_part)]
        dst = attn_ref.at[:, columns(t - core + yh, q_width)]
        own = jnp.logical_and(group == c, p == t)

        @pl.when(own)
        def _():
            near(src, dst, recv_sem.at[10]).start()

        @pl.when(jnp.logical_not(own))
        def _():
            remote(src, dst, send_sem.at[10], recv_sem.at[10], group, p).start()

        return carry

    lax.fori_loop(0, n_tp, send_attn, 0)

    wait_for(enter_all, recv_sem.at[9])
    wait_for(gates, recv_sem.at[4])
    mid_high, mid_low = halves(grown[rows - 1 : rows, :] * enter_all[...].astype(F32) + middle[...])
    next_high[...] = mid_high
    next_low[...] = mid_low
    block = rows // 2

    def gate_rows(k, carry):
        at = pl.ds(pl.multiple_of(k * block, 16), block)
        out_high, out_low = halves(mixed[at, out_cols])

        def close(carried):
            y = inner[at, :] + grown[at, :] * carried
            gated = y * silu(gates[at, :].astype(F32))
            inner[at, :] = gated
            square = jnp.sum(gated * gated, axis=1, keepdims=True)
            squares[at, :] = jnp.broadcast_to(square, (block, 128))

        @pl.when(k < 2)
        def _():
            close(fast_dot(out_high, enter_all[...]) + fast_dot(out_low, enter_all[...]))

        @pl.when(k >= 2)
        def _():
            first_part = fast_dot(out_high, next_high[...]) + fast_dot(out_low, next_high[...])
            close(first_part + fast_dot(out_high, next_low[...]))

        return carry

    lax.fori_loop(0, 4, gate_rows, 0)
    square_out[...] = squares[...].T[:8]
    square_copy = remote(
        square_out, square_in, send_sem.at[12], recv_sem.at[13], 2 * z + 1 - yh, t
    )
    square_copy.start()
    square_copy.wait_recv()
    total = square_out[0:1, :] + square_in[0:1, :]
    norm_row = lax.rsqrt(total / inner_width + 1e-05)
    squares[...] = jnp.broadcast_to(norm_row, (128, both_rows)).T
    out_at = pl.ds(pl.multiple_of(t * inner_width + yh * half_width, 128), half_width)
    gain = gain_ref[:, pl.ds(pl.multiple_of(yh * half_width, 128), half_width)]

    def normed(k, carry):
        part = lax.rem(k + 2 * yh, 4)
        at = pl.ds(pl.multiple_of(part * block, 16), block)
        mamba_loc[at, :] = (inner[at, :] * widened(squares[at, :], half_width) * gain).astype(BF16)
        return carry

    lax.fori_loop(0, 4, normed, 0)

    def send_mamba(k, carry):
        half, p = plane_peer(k)
        src = mamba_loc.at[pl.ds(pl.multiple_of(half * rows + p * row_part, 16), row_part)]
        remote(src, mamba_ref.at[:, out_at], send_sem.at[11], recv_sem.at[11], 2 * z + half, p).start()
        return carry

    lax.fori_loop(1, 2 * n_tp, send_mamba, 0)
    near(mamba_loc.at[plane_rows], mamba_ref.at[:, out_at], recv_sem.at[11]).start()

    wait_for(attn_ref, recv_sem.at[10])
    wait_for(mamba_ref, recv_sem.at[11])
    others = (n_tp - 1) * row_part
    plane_others = pl.ds(0, both_rows - row_part)
    wait_for(chan.at[plane_others], send_sem.at[0])
    wait_for(steps.at[plane_others], send_sem.at[1])
    wait_for(gates.at[plane_others], send_sem.at[4])
    wait_for(mamba_loc.at[plane_others], send_sem.at[11])
    square_copy.wait_send()
    for ref, which in ((raw_kv, 2), (raw_q, 3), (attn_loc, 10)):

        @pl.when(on_diagonal)
        def _(ref=ref, which=which):
            wait_for(ref.at[pl.ds(0, others)], send_sem.at[which])

        @pl.when(jnp.logical_not(on_diagonal))
        def _(ref=ref, which=which):
            wait_for(ref, send_sem.at[which])

    @pl.when(jnp.logical_not(on_diagonal))
    def _():
        wait_for(cache_ref, send_sem.at[5])

    halo_copy.wait_send()
    wait_for(state_all.at[pl.ds(0, nz - 1)], send_sem.at[7])
    wait_for(enter_out.at[pl.ds(0, nz - 1)], send_sem.at[9])
    for which in range(2):
        for way in (1, -1):
            for step in range(far):
                ring_copy(which, way, step, False).wait_send()
        sib_copy(which, 1, 0, False).wait_send()
        for dist in range(1, far + 1):
            for way in (1, -1):
                sib_copy(which, way, dist, False).wait_send()


def group_of_partner(z, yh):
    return 2 * z + yh


def local(
    queries,
    keyvals,
    cache_kv,
    conv_input,
    gate_input,
    dt_raw,
    conv_weight,
    conv_bias,
    dt_bias,
    decay_log,
    skip_weight,
    norm_gain,
    ssm_init,
    conv_init,
    prompt_start,
    cache_length,
):
    n_ctx = lax.axis_size("ctx")
    n_tp = lax.axis_size("tp")
    c = lax.axis_index("ctx")
    t = lax.axis_index("tp")
    head = cache_kv.shape[1] // 2
    row_part = queries.shape[0]
    rows = row_part * n_tp
    n_heads, phead, n_state = ssm_init.shape
    inner_width = n_heads * phead
    conv_width = conv_weight.shape[1]
    q_width = queries.shape[1] // n_tp
    cache_rows = cache_kv.shape[0]
    far = n_ctx // 4
    half = inner_width // 2
    own_width = half + 2 * n_state

    group = (c // 2) * 2 + t % 2
    half_width = head // 2
    lane_index = (jnp.arange(head, dtype=jnp.int32) % half_width).astype(F32)
    inverse = jnp.power(F32(10000.0), -lane_index / half_width)
    positions = prompt_start[0] + group * rows + jnp.arange(rows, dtype=jnp.int32)
    angles = positions.astype(F32)[:, None] * inverse[None, :]
    hbm = pl.BlockSpec(memory_space=pl.ANY)
    vmem = pl.BlockSpec(memory_space=pltpu.VMEM)
    smem = pl.BlockSpec(memory_space=pltpu.SMEM)
    dma = pltpu.SemaphoreType.DMA
    local_rows = rows * q_width // head
    return pl.pallas_call(
        functools.partial(kernel, n_ctx, n_tp, phead),
        out_shape=(
            jax.ShapeDtypeStruct(queries.shape, BF16),
            jax.ShapeDtypeStruct(gate_input.shape, BF16),
        ),
        in_specs=[smem] + [hbm] * 7 + [vmem] * 9,
        out_specs=(hbm, hbm),
        scratch_shapes=[
            pltpu.VMEM((n_ctx, cache_rows, 2 * head), BF16),
            pltpu.VMEM((n_ctx, rows, 2 * head), BF16),
            pltpu.VMEM((rows, 2 * head), BF16),
            pltpu.VMEM((rows, q_width), BF16),
            pltpu.VMEM((2 * rows, own_width), BF16),
            pltpu.VMEM((PAD, own_width), BF16),
            pltpu.VMEM((2 * rows, half), BF16),
            pltpu.VMEM((2 * rows, min(128, dt_raw.shape[1])), BF16),
            pltpu.VMEM((2 * rows, own_width), F32),
            pltpu.VMEM((2 * rows, half), BF16),
            pltpu.VMEM((2 * rows, half), BF16),
            pltpu.VMEM((2 * rows, half), F32),
            pltpu.VMEM((2 * rows, half), F32),
            pltpu.VMEM((2 * rows, half), F32),
            pltpu.VMEM((2 * rows, half), F32),
            pltpu.VMEM((2 * rows, half), F32),
            pltpu.VMEM((8, half), F32),
            pltpu.VMEM((128, 2 * rows), F32),
            pltpu.VMEM((2, rows, rows), F32),
            pltpu.VMEM((n_ctx // 2, n_state // 2 + PAD, 128), BF16),
            pltpu.VMEM((n_ctx // 2, n_state // 2 + PAD, 128), BF16),
            pltpu.VMEM((n_ctx // 2, n_state // 2, 128), BF16),
            pltpu.VMEM((n_state, half), BF16),
            pltpu.VMEM((local_rows, 2 * head), BF16),
            pltpu.VMEM((local_rows, 128), F32),
            pltpu.VMEM((local_rows, 2 * head), F32),
            pltpu.VMEM((rows, q_width), BF16),
            pltpu.VMEM((2 * rows, half), BF16),
            pltpu.VMEM((PAD, conv_width), F32),
            pltpu.VMEM((8, 128), F32),
            pltpu.VMEM((128 // phead, phead, n_state // 2), F32),
            pltpu.VMEM((n_state, half), F32),
            pltpu.VMEM((n_state, half), BF16),
            pltpu.VMEM((n_state, half), BF16),
            pltpu.VMEM((2 * rows, 128), F32),
            pltpu.VMEM((8, 2 * rows), F32),
            pltpu.VMEM((8, 2 * rows), F32),
            dma((13,)),
            dma((14,)),
            dma((4 * far,)),
            dma((4 * far,)),
            dma((4 * (far + 1),)),
            dma((4 * (far + 1),)),
        ],
        compiler_params=pltpu.CompilerParams(
            collective_id=0, has_side_effects=True, vmem_limit_bytes=62 * 1024 * 1024
        ),
        cost_estimate=pl.CostEstimate(
            flops=8 * 10**9, bytes_accessed=6 * 10**6, transcendentals=14 * 10**6
        ),
    )(
        cache_length,
        queries,
        keyvals,
        cache_kv,
        conv_input,
        gate_input,
        dt_raw,
        ssm_init,
        conv_init,
        conv_weight,
        conv_bias,
        dt_bias[None, :],
        decay_log[None, :],
        skip_weight[None, :],
        norm_gain[None, :],
        jnp.cos(angles),
        jnp.sin(angles),
    )


def solution(mesh):
    return jax.shard_map(
        local,
        mesh=mesh,
        in_specs=(
            P(("ctx", "tp"), None),
            P(("ctx", "tp"), None),
            P("ctx", "tp"),
            P(("ctx", "tp"), None),
            P(("ctx", "tp"), None),
            P(("ctx", "tp"), None),
            P(None, "tp"),
            P("tp"),
            P("tp"),
            P("tp"),
            P("tp"),
            P("tp"),
            P("tp", None, None),
            P(None, "tp"),
            P(),
            P(),
        ),
        out_specs=(P(("ctx", "tp"), None), P(("ctx", "tp"), None)),
        check_vma=False,
    )
```

```python
import functools
import math

import jax
import jax.numpy as jnp
from jax import lax
from jax.experimental import pallas as pl
from jax.experimental.pallas import tpu as pltpu
from jax.sharding import PartitionSpec as P

HIGHEST = lax.Precision.HIGHEST
F32 = jnp.float32
BF16 = jnp.bfloat16
MESH = pl.DeviceIdType.MESH
PAD = 16
FLOOR = -1e20
HIDDEN = -1e30


def exact_dot(a, b, dims=(((1,), (0,)), ((), ()))):
    return lax.dot_general(a, b, dims, precision=HIGHEST, preferred_element_type=F32)


def fast_dot(a, b, dims=(((1,), (0,)), ((), ()))):
    return lax.dot_general(a, b, dims, preferred_element_type=F32)


def halves(a):
    high = a.astype(BF16)
    return high, (a - high.astype(F32)).astype(BF16)


def silu(a):
    return a / (1.0 + jnp.exp(-a))


def widened(a, width):
    return jnp.tile(a, (1, -(-width // a.shape[1])))[:, :width]


def kernel(
    n_ctx,
    n_tp,
    phead,
    length_ref,
    q_ref,
    kv_ref,
    cache_ref,
    conv_ref,
    gate_ref,
    dt_ref,
    init_ref,
    first_ref,
    tap_ref,
    bias_ref,
    dt_bias_ref,
    rate_ref,
    skip_ref,
    gain_ref,
    cos_ref,
    sin_ref,
    attn_ref,
    mamba_ref,
    kvc,
    kvp,
    raw_kv,
    raw_q,
    chan,
    halo,
    gates,
    steps,
    mixed,
    x_high,
    x_low,
    inner,
    grown,
    cum_wide,
    step_wide,
    toward_wide,
    skip_wide,
    cum_rows,
    contact,
    state_out,
    state_all,
    enter_out,
    enter_all,
    queries,
    top,
    acc,
    attn_loc,
    mamba_loc,
    first,
    small_ref,
    init_piece,
    middle,
    next_high,
    next_low,
    squares,
    square_out,
    square_in,
    send_sem,
    recv_sem,
    ring_send,
    ring_recv,
    sib_send,
    sib_recv,
):
    c = lax.axis_index("ctx")
    t = lax.axis_index("tp")
    nz = n_ctx // 2
    far = nz // 2
    z = c // 2
    yh = lax.rem(c, 2)
    core = lax.rem(t, 2)
    group = 2 * z + core
    row_part = q_ref.shape[0]
    rows = row_part * n_tp
    q_width = raw_q.shape[1]
    kv_width = raw_kv.shape[1]
    head = kv_width // 2
    local_q = q_width // head
    conv_width = tap_ref.shape[1]
    inner_width = gain_ref.shape[1]
    n_state = (conv_width - inner_width) // 2
    half_width = gates.shape[1]
    own_width = chan.shape[1]
    both_rows = 2 * rows
    cache_rows = kvc.shape[1]
    my_rows = pl.ds(pl.multiple_of(t * row_part, 16), row_part)
    on_diagonal = yh == core
    plane_rows = pl.ds(pl.multiple_of(yh * rows + t * row_part, 16), row_part)

    def columns(index, width):
        return pl.ds(pl.multiple_of(index * width, 128), width)

    def remote(src, dst, s_sem, r_sem, ctx_id, tp_id):
        return pltpu.make_async_remote_copy(
            src_ref=src,
            dst_ref=dst,
            send_sem=s_sem,
            recv_sem=r_sem,
            device_id=(ctx_id, tp_id),
            device_id_type=MESH,
        )

    def near(src, dst, sem):
        return pltpu.make_async_copy(src, dst, sem)

    def wait_for(ref, sem):
        near(ref, ref, sem).wait()

    barrier = pltpu.get_barrier_semaphore()

    def greet(ctx_id, tp_id):
        pl.semaphore_signal(barrier, inc=1, device_id=(ctx_id, tp_id), device_id_type=MESH)

    def greet_plane(k, carry):
        greet(2 * z + 1 - yh, k)

        @pl.when(k > 0)
        def _():
            greet(c, lax.rem(t + k, n_tp))

        return carry

    lax.fori_loop(0, n_tp, greet_plane, 0)

    def greet_line(k, carry):
        greet(2 * lax.rem(z + k, nz) + yh, t)
        return carry

    lax.fori_loop(1, nz, greet_line, 0)
    pl.semaphore_wait(barrier, 2 * n_tp - 1 + nz - 1)

    half_state = n_state // 2
    own_rows = pl.ds(pl.multiple_of(lax.rem(z, 2) * half_state, 128), half_state)
    own_cols = columns(z // 2, 128)
    pair = 128 // phead
    n_heads = dt_bias_ref.shape[1]
    init_copy = near(
        init_ref.at[pl.ds(yh * (n_heads // 2) + (z // 2) * pair, pair), :, own_rows],
        init_piece,
        recv_sem.at[8],
    )
    init_copy.start()

    @pl.when(on_diagonal)
    def _():
        near(cache_ref, kvc.at[group], recv_sem.at[5]).start()

    @pl.when(jnp.logical_not(on_diagonal))
    def _():
        remote(
            cache_ref, kvc.at[group_of_partner(z, yh)], send_sem.at[5], recv_sem.at[5], group, t - core + yh
        ).start()

    def send_heads(src_ref, width, dst_ref, which):
        def body(k, carry):
            h = lax.rem(t + k, n_tp)
            to_ctx = 2 * z + lax.rem(h, 2)
            to_tp = (h // 2) * 2 + yh
            own = jnp.logical_and(to_ctx == c, to_tp == t)
            src = src_ref.at[:, columns(h, width)]
            dst = dst_ref.at[my_rows]

            @pl.when(own)
            def _():
                near(src, dst, recv_sem.at[which]).start()

            @pl.when(jnp.logical_not(own))
            def _():
                remote(src, dst, send_sem.at[which], recv_sem.at[which], to_ctx, to_tp).start()

            return carry

        lax.fori_loop(0, n_tp, body, 0)

    is_last = jnp.logical_and(t == n_tp - 1, yh == 1)
    conv_sem = recv_sem.at[jnp.where(is_last, 12, 0)]
    dt_width = steps.shape[1]
    per_dt = dt_width // n_heads

    def mixer_pieces(half, p):
        begin = p * conv_width
        return (
            (dt_ref.at[:, columns(p // per_dt, dt_width)], steps.at[plane_rows], 1),
            (
                conv_ref.at[:, pl.ds(pl.multiple_of(begin + half * half_width, 128), half_width)],
                chan.at[plane_rows, pl.ds(0, half_width)],
                0,
            ),
            (
                conv_ref.at[:, pl.ds(pl.multiple_of(begin + inner_width, 128), 2 * n_state)],
                chan.at[plane_rows, pl.ds(half_width, 2 * n_state)],
                0,
            ),
        )

    def gate_piece(half, p):
        return gate_ref.at[:, pl.ds(pl.multiple_of(p * inner_width + half * half_width, 128), half_width)]

    def plane_peer(k):
        return lax.rem(yh + k // n_tp, 2), lax.rem(t + k, n_tp)

    def send_mixer(k, carry):
        half, p = plane_peer(k)
        for src, dst, which in mixer_pieces(half, p):
            to_sem = recv_sem.at[which] if which else conv_sem
            remote(src, dst, send_sem.at[which], to_sem, 2 * z + half, p).start()
        return carry

    def send_gate(k, carry):
        half, p = plane_peer(k)
        remote(
            gate_piece(half, p), gates.at[plane_rows], send_sem.at[4], recv_sem.at[4], 2 * z + half, p
        ).start()
        return carry

    send_heads(kv_ref, kv_width, raw_kv, 2)
    lax.fori_loop(1, 2 * n_tp, send_mixer, 0)
    for src, dst, which in mixer_pieces(yh, t):
        near(src, dst, recv_sem.at[which] if which else conv_sem).start()

    def region(buf, way, dist, parity, cut):
        slot = 2 * lax.rem(z - way * dist + nz, nz) + parity
        if not cut:
            return buf.at[slot]
        half = buf.shape[1] // 2
        return buf.at[slot, pl.ds(0 if way > 0 else half, half)]

    bufs = (kvc, kvp)

    def ring_copy(which, way, step, arriving):
        cut = step + 1 == far
        piece = region(bufs[which], way, step + 1 if arriving else step, core, cut)
        at = (which * 2 + (way < 0)) * far + step
        return remote(
            piece,
            piece,
            ring_send.at[at],
            ring_recv.at[at],
            2 * lax.rem(z + way + nz, nz) + yh,
            t,
        )

    def sib_copy(which, way, dist, arriving):
        cut = dist == far
        piece = region(bufs[which], way, dist, 1 - core if arriving else core, cut)
        at = (which * 2 + (way < 0)) * (far + 1) + dist
        return remote(piece, piece, sib_send.at[at], sib_recv.at[at], c, t + 1 - 2 * core)

    def ring_begin(which):
        for way in (1, -1):
            ring_copy(which, way, 0, False).start()
        sib_copy(which, 1, 0, False).start()

    def ring_advance(which, step):
        for way in (1, -1):
            ring_copy(which, way, step, True).wait_recv()
            if step + 1 < far:
                ring_copy(which, way, step + 1, False).start()
        for way in (1, -1):
            sib_copy(which, way, step + 1, False).start()

    def sib_wait(which, dist):
        for way in (1, -1) if dist else (1,):
            sib_copy(which, way, dist, True).wait_recv()

    wait_for(kvc.at[group], recv_sem.at[5])
    ring_begin(0)

    lane = lax.broadcasted_iota(jnp.int32, (rows, head), 1)
    sine = jnp.where(lane < head // 2, -sin_ref[...], sin_ref[...])
    cosine = cos_ref[...]

    def rotated(a):
        a = a.astype(F32)
        return (a * cosine + pltpu.roll(a, head // 2, 1) * sine).astype(BF16)

    wait_for(raw_kv, recv_sem.at[2])
    kvp[group] = jnp.concatenate([rotated(raw_kv[:, :head]), raw_kv[:, head:]], axis=1)
    ring_begin(1)

    first[...] = jnp.zeros(first.shape, F32)
    first[pl.ds(PAD - first_ref.shape[0], first_ref.shape[0]), :] = first_ref[...].astype(F32)
    small_ref[...] = jnp.zeros(small_ref.shape, F32)
    small_ref[0:1, 0:n_heads] = dt_bias_ref[...]
    small_ref[1:2, 0:n_heads] = rate_ref[...]
    small_ref[2:3, 0:n_heads] = skip_ref[...]
    half_heads = n_heads // 2
    to_lane = lax.broadcasted_iota(jnp.int32, (128, 128), 1)
    of_half = jnp.logical_and(
        lax.broadcasted_iota(jnp.int32, (128, 128), 0) == yh * half_heads + to_lane, to_lane < half_heads
    )
    small = exact_dot(small_ref[...], of_half.astype(F32))
    pick = lax.broadcasted_iota(jnp.int32, (dt_width, 128), 0) == (
        lax.rem(t, per_dt) * n_heads
        + yh * half_heads
        + lax.broadcasted_iota(jnp.int32, (dt_width, 128), 1)
    )
    row_at = lax.broadcasted_iota(jnp.int32, (rows, rows), 0)
    col_at = lax.broadcasted_iota(jnp.int32, (rows, rows), 1)
    causal = row_at >= col_at
    wide_at = 2 * 128
    wait_for(steps, recv_sem.at[1])
    raw_step = fast_dot(steps[...], pick.astype(F32).astype(BF16)) + small[0:1]
    step_size = jnp.maximum(raw_step, 0.0) + jnp.log1p(jnp.exp(-jnp.abs(raw_step)))
    log_decay = -jnp.exp(small[1:2]) * step_size
    tri = causal.astype(F32)
    cumulative = jnp.concatenate(
        [exact_dot(tri, log_decay[:rows]), exact_dot(tri, log_decay[rows:])], axis=0
    )
    cum_rows[...] = cumulative.T

    def spread_out(j, carry):
        cols = columns(j, wide_at)
        spread = lax.broadcasted_iota(jnp.int32, (128, wide_at), 0) == (
            j * (wide_at // phead) + lax.broadcasted_iota(jnp.int32, (128, wide_at), 1) // phead
        )
        spread = spread.astype(F32)
        for part in range(2):
            at = pl.ds(part * rows, rows)
            here = slice(part * rows, part * rows + rows)
            cum_here = exact_dot(cumulative[here], spread)
            step_here = exact_dot(step_size[here], spread)
            cum_wide[at, cols] = cum_here
            grown[at, cols] = jnp.exp(cum_here)
            step_wide[at, cols] = step_here
            toward_wide[at, cols] = step_here * jnp.exp(cum_here[rows - 1 : rows] - cum_here)
        skip_wide[:, cols] = exact_dot(small, spread)
        return carry

    lax.fori_loop(0, half_width // wide_at, spread_out, 0)
    ring_advance(0, 0)
    ring_advance(1, 0)

    last_rows = pl.ds(both_rows - PAD, PAD)
    wait_for(chan.at[last_rows], recv_sem.at[12])
    halo_copy = remote(
        chan.at[last_rows], halo, send_sem.at[6], recv_sem.at[6], 2 * lax.rem(z + 1, nz) + yh, t
    )
    halo_copy.start()
    wait_for(chan.at[pl.ds(0, both_rows - row_part)], recv_sem.at[0])
    send_heads(q_ref, q_width, raw_q, 3)
    halo_copy.wait_recv()
    n_taps = tap_ref.shape[0]
    piece = 256

    def convolve(j, carry):
        cols = columns(j, piece)
        begin = j * piece + jnp.where(j * piece < half_width, yh * half_width, inner_width - half_width)
        from_cols = pl.ds(pl.multiple_of(begin, 128), piece)
        before = jnp.where(z == 0, first[:, from_cols], halo[:, cols].astype(F32))
        wide = jnp.concatenate([before, chan[:, cols].astype(F32)], axis=0)
        total = bias_ref[from_cols][None, :]
        for tap in range(n_taps):
            start = PAD - (n_taps - 1) + tap
            total = total + tap_ref[pl.ds(tap, 1), from_cols] * wide[start : start + both_rows]
        mixed[:, cols] = silu(total)
        return carry

    lax.fori_loop(0, (half_width + n_state) // piece, convolve, 0)
    ring_advance(0, 1)
    in_cols = pl.ds(half_width, n_state)
    out_cols = pl.ds(half_width + n_state, n_state)

    def states(k, carry):
        j = lax.rem(k + z // far, half_width // wide_at)
        cols = columns(j, wide_at)
        fresh = []
        for part in range(2):
            at = pl.ds(part * rows, rows)
            here = mixed[at, cols]
            high, low = halves(here * step_wide[at, cols])
            x_high[at, cols] = high
            x_low[at, cols] = low
            toward = here * toward_wide[at, cols]
            fresh.append(exact_dot(mixed[at, in_cols], toward, (((0,), (0,)), ((), ()))))
        middle[:, cols] = fresh[0]
        later = grown[both_rows - 1 : both_rows, cols]
        fresh = later * fresh[0] + fresh[1]
        fresh = fresh.astype(BF16)
        decay = grown[rows - 1 : rows, cols] * later
        decay_1 = decay.astype(BF16).astype(F32)
        decay_2 = (decay - decay_1).astype(BF16).astype(F32)
        decay_3 = decay - decay_1 - decay_2
        at = lax.broadcasted_iota(jnp.int32, (PAD, wide_at), 0)
        decays = jnp.where(at == 0, decay_1, jnp.where(at == 1, decay_2, jnp.where(at == 2, decay_3, 0.0)))
        decays = decays.astype(BF16)
        for k in range(2 * wide_at // 128):
            i = j * (2 * wide_at // 128) + k
            lanes = slice(k // 2 * 128, k // 2 * 128 + 128)
            start = k % 2 * half_state
            state_out[i, :half_state] = fresh[start : start + half_state, lanes]
            state_out[i, half_state:] = decays[:, lanes]

            @pl.when(i == z)
            def _(i=i):
                near(state_out.at[i], state_all.at[z], recv_sem.at[7]).start()

            @pl.when(i != z)
            def _(i=i):
                remote(
                    state_out.at[i], state_all.at[z], send_sem.at[7], recv_sem.at[7], 2 * i + yh, t
                ).start()

        return carry

    lax.fori_loop(0, half_width // wide_at, states, 0)
    near(gate_piece(yh, t), gates.at[plane_rows], recv_sem.at[4]).start()
    lax.fori_loop(1, 2 * n_tp, send_gate, 0)
    ring_advance(1, 1)
    lax.fori_loop((half_width + n_state) // piece, own_width // piece, convolve, 0)

    for part in range(2):
        at = pl.ds(part * rows, rows)
        contact[part] = exact_dot(mixed[at, out_cols], mixed[at, in_cols], (((1,), (1,)), ((), ())))
    pair_lane = lax.broadcasted_iota(jnp.int32, (rows, 128), 1)
    pairs = half_width // 128

    def within(k, carry):
        part = k // pairs
        j = lax.rem(k, pairs)
        at = pl.ds(pl.multiple_of(part * rows, 16), rows)
        cols = columns(j, 128)
        cum_pair = cum_wide[at, cols]
        both = jnp.concatenate([x_high[at, cols], x_low[at, cols]], axis=1)
        pieces = []
        for i in range(2):
            row = cum_rows[pl.ds(2 * j + i, 1), :]
            row = jnp.where(part == 0, row[:, :rows], row[:, rows:])
            gap = cum_pair[:, i * phead : i * phead + 1] - row
            mixing = contact[part] * jnp.exp(jnp.where(causal, gap, HIDDEN))
            high, low = halves(mixing)
            product = fast_dot(high, both)
            pieces.append(product[:, :128] + product[:, 128:] + fast_dot(low, both[:, :128]))
        inner[at, cols] = mixed[at, cols] * skip_wide[2:3, cols] + jnp.where(
            pair_lane < phead, pieces[0], pieces[1]
        )
        return carry

    lax.fori_loop(0, 2 * pairs, within, 0)
    ring_advance(0, 2)

    wait_for(raw_q, recv_sem.at[3])
    mark = (lax.broadcasted_iota(jnp.int32, (rows, head), 1) == 0).astype(F32).astype(BF16)
    for h in range(local_q):
        part = rotated(raw_q[:, h * head : (h + 1) * head])
        queries[pl.ds(h * rows, rows), :] = jnp.concatenate([part, mark], axis=1)
    top[...] = jnp.full(top.shape, FLOOR, F32)
    acc[...] = jnp.zeros(acc.shape, F32)
    factor = math.log2(math.e) / math.sqrt(head)
    length = length_ref[0]
    pair_rows = 2 * cache_rows

    def update(key, value, diagonal):
        for h in range(local_q):
            at = pl.ds(h * rows, rows)
            score = fast_dot(queries[at, :], key, (((1,), (1,)), ((), ())))
            if diagonal:
                shape = (rows, 2 * rows)
                seen = lax.broadcasted_iota(jnp.int32, shape, 1) <= (
                    core * rows + lax.broadcasted_iota(jnp.int32, shape, 0)
                )
                masked = jnp.where(seen, score[:, pair_rows:], HIDDEN)
                score = jnp.concatenate([score[:, :pair_rows], masked], axis=1)
            old = top[at, :]
            new = jnp.maximum(old, jnp.max(score, axis=1, keepdims=True))
            top[at, :] = new
            weight = jnp.exp2((score - widened(new, score.shape[1])) * factor)
            scale = jnp.exp2((old - new) * factor)
            acc[at, :] = acc[at, :] * widened(scale, 2 * head) + fast_dot(weight.astype(BF16), value)

    def attend(place):
        def run(prompt, diagonal):
            lanes = lax.broadcasted_iota(jnp.int32, (pair_rows, head), 1)
            slots = place * pair_rows + lax.broadcasted_iota(jnp.int32, (pair_rows, head), 0)
            hide = jnp.where(jnp.logical_and(lanes == 0, slots >= length), HIDDEN, 0.0).astype(BF16)
            cached = kvc[pl.ds(2 * place, 2)].reshape(pair_rows, 2 * head)
            key, value = cached[:, :head], cached[:, head:]
            if prompt:
                more = kvp[pl.ds(2 * place, 2)].reshape(2 * rows, 2 * head)
                key = jnp.concatenate([key, more[:, :head]], axis=0)
                value = jnp.concatenate([value, more[:, head:]], axis=0)
                hide = jnp.concatenate([hide, jnp.zeros((2 * rows, head), BF16)], axis=0)
            ones = jnp.ones(value.shape, BF16)
            update(
                jnp.concatenate([key, hide], axis=1), jnp.concatenate([value, ones], axis=1), diagonal
            )

        pl.when(place < z)(functools.partial(run, True, False))
        pl.when(place == z)(functools.partial(run, True, True))
        pl.when(place > z)(functools.partial(run, False, False))

    def pass_states():
        wait_for(state_all, recv_sem.at[7])
        init_copy.wait()

        def scan_group(i, state):
            enter_out[i] = state.astype(BF16)
            parts = state_all[i, half_state:].astype(F32)
            decay = parts[0:1] + parts[1:2] + parts[2:3]
            return decay * state + state_all[i, :half_state].astype(F32)

        lax.fori_loop(0, nz, scan_group, init_piece[...].reshape(128, half_state).T)

        def send_enter(k, carry):
            i = lax.rem(z + k, nz)
            remote(
                enter_out.at[i],
                enter_all.at[own_rows, own_cols],
                send_sem.at[9],
                recv_sem.at[9],
                2 * i + yh,
                t,
            ).start()
            return carry

        near(enter_out.at[z], enter_all.at[own_rows, own_cols], recv_sem.at[9]).start()
        lax.fori_loop(1, nz, send_enter, 0)

    block = rows // 2
    square_copy = remote(square_out, square_in, send_sem.at[12], recv_sem.at[13], 2 * z + 1 - yh, t)

    def end_mixer():
        wait_for(enter_all, recv_sem.at[9])
        wait_for(gates, recv_sem.at[4])
        mid_high, mid_low = halves(grown[rows - 1 : rows, :] * enter_all[...].astype(F32) + middle[...])
        next_high[...] = mid_high
        next_low[...] = mid_low

        def gate_rows(k, carry):
            at = pl.ds(pl.multiple_of(k * block, 16), block)
            out_high, out_low = halves(mixed[at, out_cols])

            def close(carried):
                y = inner[at, :] + grown[at, :] * carried
                gated = y * silu(gates[at, :].astype(F32))
                inner[at, :] = gated
                square = jnp.sum(gated * gated, axis=1, keepdims=True)
                squares[at, :] = jnp.broadcast_to(square, (block, 128))

            @pl.when(k < 2)
            def _():
                close(fast_dot(out_high, enter_all[...]) + fast_dot(out_low, enter_all[...]))

            @pl.when(k >= 2)
            def _():
                first_part = fast_dot(out_high, next_high[...]) + fast_dot(out_low, next_high[...])
                close(first_part + fast_dot(out_high, next_low[...]))

            return carry

        lax.fori_loop(0, 4, gate_rows, 0)
        square_out[...] = squares[...].T[:8]
        square_copy.start()

    def send_mixed():
        square_copy.wait_recv()
        total = square_out[0:1, :] + square_in[0:1, :]
        norm_row = lax.rsqrt(total / inner_width + 1e-05)
        squares[...] = jnp.broadcast_to(norm_row, (128, both_rows)).T
        out_at = pl.ds(pl.multiple_of(t * inner_width + yh * half_width, 128), half_width)
        gain = gain_ref[:, pl.ds(pl.multiple_of(yh * half_width, 128), half_width)]

        def normed(k, carry):
            part = lax.rem(k + 2 * yh, 4)
            at = pl.ds(pl.multiple_of(part * block, 16), block)
            mamba_loc[at, :] = (inner[at, :] * widened(squares[at, :], half_width) * gain).astype(BF16)
            return carry

        lax.fori_loop(0, 4, normed, 0)

        def send_mamba(k, carry):
            half, p = plane_peer(k)
            src = mamba_loc.at[pl.ds(pl.multiple_of(half * rows + p * row_part, 16), row_part)]
            remote(src, mamba_ref.at[:, out_at], send_sem.at[11], recv_sem.at[11], 2 * z + half, p).start()
            return carry

        lax.fori_loop(1, 2 * n_tp, send_mamba, 0)
        near(mamba_loc.at[plane_rows], mamba_ref.at[:, out_at], recv_sem.at[11]).start()

    def sib_wait_both(dist):
        sib_wait(0, dist)
        sib_wait(1, dist)

    events = {
        0: (functools.partial(sib_wait_both, 0), functools.partial(sib_wait_both, 1)),
        1: (pass_states,),
        2: (functools.partial(ring_advance, 1, 2),),
        3: (functools.partial(sib_wait_both, 2), functools.partial(ring_advance, 0, 3)),
        5: (functools.partial(sib_wait_both, 3), end_mixer),
        6: (functools.partial(ring_advance, 1, 3), send_mixed),
        7: (functools.partial(sib_wait_both, 4),),
    }

    def attend_next(k, carry):
        for at, calls in events.items():

            @pl.when(k == at)
            def _(calls=calls):
                for call in calls:
                    call()

        back = lax.rem(k, 2) == 0
        attend(lax.rem(jnp.where(back, z + nz - k // 2, z + (k + 1) // 2), nz))
        return carry

    lax.fori_loop(0, nz, attend_next, 0)
    for h in range(local_q):
        found = acc[pl.ds(h * rows, rows), :]
        attn_loc[:, h * head : (h + 1) * head] = (found[:, :head] / found[:, head:]).astype(BF16)

    def send_attn(p, carry):
        src = attn_loc.at[pl.ds(pl.multiple_of(p * row_part, 16), row_part)]
        dst = attn_ref.at[:, columns(t - core + yh, q_width)]
        own = jnp.logical_and(group == c, p == t)

        @pl.when(own)
        def _():
            near(src, dst, recv_sem.at[10]).start()

        @pl.when(jnp.logical_not(own))
        def _():
            remote(src, dst, send_sem.at[10], recv_sem.at[10], group, p).start()

        return carry

    lax.fori_loop(0, n_tp, send_attn, 0)

    wait_for(attn_ref, recv_sem.at[10])
    wait_for(mamba_ref, recv_sem.at[11])
    others = (n_tp - 1) * row_part
    plane_others = pl.ds(0, both_rows - row_part)
    wait_for(chan.at[plane_others], send_sem.at[0])
    wait_for(steps.at[plane_others], send_sem.at[1])
    wait_for(gates.at[plane_others], send_sem.at[4])
    wait_for(mamba_loc.at[plane_others], send_sem.at[11])
    square_copy.wait_send()
    for ref, which in ((raw_kv, 2), (raw_q, 3), (attn_loc, 10)):

        @pl.when(on_diagonal)
        def _(ref=ref, which=which):
            wait_for(ref.at[pl.ds(0, others)], send_sem.at[which])

        @pl.when(jnp.logical_not(on_diagonal))
        def _(ref=ref, which=which):
            wait_for(ref, send_sem.at[which])

    @pl.when(jnp.logical_not(on_diagonal))
    def _():
        wait_for(cache_ref, send_sem.at[5])

    halo_copy.wait_send()
    wait_for(state_all.at[pl.ds(0, nz - 1)], send_sem.at[7])
    wait_for(enter_out.at[pl.ds(0, nz - 1)], send_sem.at[9])
    for which in range(2):
        for way in (1, -1):
            for step in range(far):
                ring_copy(which, way, step, False).wait_send()
        sib_copy(which, 1, 0, False).wait_send()
        for dist in range(1, far + 1):
            for way in (1, -1):
                sib_copy(which, way, dist, False).wait_send()


def group_of_partner(z, yh):
    return 2 * z + yh


def local(
    queries,
    keyvals,
    cache_kv,
    conv_input,
    gate_input,
    dt_raw,
    conv_weight,
    conv_bias,
    dt_bias,
    decay_log,
    skip_weight,
    norm_gain,
    ssm_init,
    conv_init,
    prompt_start,
    cache_length,
):
    n_ctx = lax.axis_size("ctx")
    n_tp = lax.axis_size("tp")
    c = lax.axis_index("ctx")
    t = lax.axis_index("tp")
    head = cache_kv.shape[1] // 2
    row_part = queries.shape[0]
    rows = row_part * n_tp
    n_heads, phead, n_state = ssm_init.shape
    inner_width = n_heads * phead
    conv_width = conv_weight.shape[1]
    q_width = queries.shape[1] // n_tp
    cache_rows = cache_kv.shape[0]
    far = n_ctx // 4
    half = inner_width // 2
    own_width = half + 2 * n_state

    group = (c // 2) * 2 + t % 2
    half_width = head // 2
    lane_index = (jnp.arange(head, dtype=jnp.int32) % half_width).astype(F32)
    inverse = jnp.power(F32(10000.0), -lane_index / half_width)
    positions = prompt_start[0] + group * rows + jnp.arange(rows, dtype=jnp.int32)
    angles = positions.astype(F32)[:, None] * inverse[None, :]
    hbm = pl.BlockSpec(memory_space=pl.ANY)
    vmem = pl.BlockSpec(memory_space=pltpu.VMEM)
    smem = pl.BlockSpec(memory_space=pltpu.SMEM)
    dma = pltpu.SemaphoreType.DMA
    local_rows = rows * q_width // head
    return pl.pallas_call(
        functools.partial(kernel, n_ctx, n_tp, phead),
        out_shape=(
            jax.ShapeDtypeStruct(queries.shape, BF16),
            jax.ShapeDtypeStruct(gate_input.shape, BF16),
        ),
        in_specs=[smem] + [hbm] * 7 + [vmem] * 9,
        out_specs=(hbm, hbm),
        scratch_shapes=[
            pltpu.VMEM((n_ctx, cache_rows, 2 * head), BF16),
            pltpu.VMEM((n_ctx, rows, 2 * head), BF16),
            pltpu.VMEM((rows, 2 * head), BF16),
            pltpu.VMEM((rows, q_width), BF16),
            pltpu.VMEM((2 * rows, own_width), BF16),
            pltpu.VMEM((PAD, own_width), BF16),
            pltpu.VMEM((2 * rows, half), BF16),
            pltpu.VMEM((2 * rows, min(128, dt_raw.shape[1])), BF16),
            pltpu.VMEM((2 * rows, own_width), F32),
            pltpu.VMEM((2 * rows, half), BF16),
            pltpu.VMEM((2 * rows, half), BF16),
            pltpu.VMEM((2 * rows, half), F32),
            pltpu.VMEM((2 * rows, half), F32),
            pltpu.VMEM((2 * rows, half), F32),
            pltpu.VMEM((2 * rows, half), F32),
            pltpu.VMEM((2 * rows, half), F32),
            pltpu.VMEM((8, half), F32),
            pltpu.VMEM((128, 2 * rows), F32),
            pltpu.VMEM((2, rows, rows), F32),
            pltpu.VMEM((n_ctx // 2, n_state // 2 + PAD, 128), BF16),
            pltpu.VMEM((n_ctx // 2, n_state // 2 + PAD, 128), BF16),
            pltpu.VMEM((n_ctx // 2, n_state // 2, 128), BF16),
            pltpu.VMEM((n_state, half), BF16),
            pltpu.VMEM((local_rows, 2 * head), BF16),
            pltpu.VMEM((local_rows, 128), F32),
            pltpu.VMEM((local_rows, 2 * head), F32),
            pltpu.VMEM((rows, q_width), BF16),
            pltpu.VMEM((2 * rows, half), BF16),
            pltpu.VMEM((PAD, conv_width), F32),
            pltpu.VMEM((8, 128), F32),
            pltpu.VMEM((128 // phead, phead, n_state // 2), F32),
            pltpu.VMEM((n_state, half), F32),
            pltpu.VMEM((n_state, half), BF16),
            pltpu.VMEM((n_state, half), BF16),
            pltpu.VMEM((2 * rows, 128), F32),
            pltpu.VMEM((8, 2 * rows), F32),
            pltpu.VMEM((8, 2 * rows), F32),
            dma((13,)),
            dma((14,)),
            dma((4 * far,)),
            dma((4 * far,)),
            dma((4 * (far + 1),)),
            dma((4 * (far + 1),)),
        ],
        compiler_params=pltpu.CompilerParams(
            collective_id=0, has_side_effects=True, vmem_limit_bytes=62 * 1024 * 1024
        ),
        cost_estimate=pl.CostEstimate(
            flops=8 * 10**9, bytes_accessed=6 * 10**6, transcendentals=14 * 10**6
        ),
    )(
        cache_length,
        queries,
        keyvals,
        cache_kv,
        conv_input,
        gate_input,
        dt_raw,
        ssm_init,
        conv_init,
        conv_weight,
        conv_bias,
        dt_bias[None, :],
        decay_log[None, :],
        skip_weight[None, :],
        norm_gain[None, :],
        jnp.cos(angles),
        jnp.sin(angles),
    )


def solution(mesh):
    return jax.shard_map(
        local,
        mesh=mesh,
        in_specs=(
            P(("ctx", "tp"), None),
            P(("ctx", "tp"), None),
            P("ctx", "tp"),
            P(("ctx", "tp"), None),
            P(("ctx", "tp"), None),
            P(("ctx", "tp"), None),
            P(None, "tp"),
            P("tp"),
            P("tp"),
            P("tp"),
            P("tp"),
            P("tp"),
            P("tp", None, None),
            P(None, "tp"),
            P(),
            P(),
        ),
        out_specs=(P(("ctx", "tp"), None), P(("ctx", "tp"), None)),
        check_vma=False,
    )
```

```python
import functools
import math

import jax
import jax.numpy as jnp
from jax import lax
from jax.experimental import pallas as pl
from jax.experimental.pallas import tpu as pltpu
from jax.sharding import PartitionSpec as P

HIGHEST = lax.Precision.HIGHEST
F32 = jnp.float32
BF16 = jnp.bfloat16
MESH = pl.DeviceIdType.MESH
PAD = 16
FLOOR = -1e20
HIDDEN = -1e30


def exact_dot(a, b, dims=(((1,), (0,)), ((), ()))):
    return lax.dot_general(a, b, dims, precision=HIGHEST, preferred_element_type=F32)


def fast_dot(a, b, dims=(((1,), (0,)), ((), ()))):
    return lax.dot_general(a, b, dims, preferred_element_type=F32)


def halves(a):
    high = a.astype(BF16)
    return high, (a - high.astype(F32)).astype(BF16)


def silu(a):
    return a / (1.0 + jnp.exp(-a))


def widened(a, width):
    return jnp.tile(a, (1, -(-width // a.shape[1])))[:, :width]


def kernel(
    n_ctx,
    n_tp,
    phead,
    length_ref,
    q_ref,
    kv_ref,
    cache_ref,
    conv_ref,
    gate_ref,
    dt_ref,
    init_ref,
    first_ref,
    tap_ref,
    bias_ref,
    dt_bias_ref,
    rate_ref,
    skip_ref,
    gain_ref,
    cos_ref,
    sin_ref,
    attn_ref,
    mamba_ref,
    kvc,
    kvp,
    raw_kv,
    raw_q,
    chan,
    halo,
    gates,
    steps,
    mixed,
    x_high,
    x_low,
    inner,
    grown,
    cum_wide,
    step_wide,
    toward_wide,
    skip_wide,
    cum_rows,
    contact,
    state_out,
    state_all,
    enter_out,
    enter_all,
    queries,
    top,
    acc,
    attn_loc,
    mamba_loc,
    first,
    small_ref,
    init_piece,
    middle,
    next_high,
    next_low,
    squares,
    square_out,
    square_in,
    send_sem,
    recv_sem,
    ring_send,
    ring_recv,
    sib_send,
    sib_recv,
):
    c = lax.axis_index("ctx")
    t = lax.axis_index("tp")
    nz = n_ctx // 2
    far = nz // 2
    z = c // 2
    yh = lax.rem(c, 2)
    core = lax.rem(t, 2)
    group = 2 * z + core
    row_part = q_ref.shape[0]
    rows = row_part * n_tp
    q_width = raw_q.shape[1]
    kv_width = raw_kv.shape[1]
    head = kv_width // 2
    local_q = q_width // head
    conv_width = tap_ref.shape[1]
    inner_width = gain_ref.shape[1]
    n_state = (conv_width - inner_width) // 2
    half_width = gates.shape[1]
    own_width = chan.shape[1]
    both_rows = 2 * rows
    cache_rows = kvc.shape[1]
    my_rows = pl.ds(pl.multiple_of(t * row_part, 16), row_part)
    on_diagonal = yh == core
    plane_rows = pl.ds(pl.multiple_of(yh * rows + t * row_part, 16), row_part)

    def columns(index, width):
        return pl.ds(pl.multiple_of(index * width, 128), width)

    def remote(src, dst, s_sem, r_sem, ctx_id, tp_id):
        return pltpu.make_async_remote_copy(
            src_ref=src,
            dst_ref=dst,
            send_sem=s_sem,
            recv_sem=r_sem,
            device_id=(ctx_id, tp_id),
            device_id_type=MESH,
        )

    def near(src, dst, sem):
        return pltpu.make_async_copy(src, dst, sem)

    def wait_for(ref, sem):
        near(ref, ref, sem).wait()

    barrier = pltpu.get_barrier_semaphore()

    def greet(ctx_id, tp_id):
        pl.semaphore_signal(barrier, inc=1, device_id=(ctx_id, tp_id), device_id_type=MESH)

    def greet_plane(k, carry):
        greet(2 * z + 1 - yh, k)

        @pl.when(k > 0)
        def _():
            greet(c, lax.rem(t + k, n_tp))

        return carry

    lax.fori_loop(0, n_tp, greet_plane, 0)

    def greet_line(k, carry):
        greet(2 * lax.rem(z + k, nz) + yh, t)
        return carry

    lax.fori_loop(1, nz, greet_line, 0)
    pl.semaphore_wait(barrier, 2 * n_tp - 1 + nz - 1)

    half_state = n_state // 2
    own_rows = pl.ds(pl.multiple_of(lax.rem(z, 2) * half_state, 128), half_state)
    own_cols = columns(z // 2, 128)
    pair = 128 // phead
    n_heads = dt_bias_ref.shape[1]
    init_copy = near(
        init_ref.at[pl.ds(yh * (n_heads // 2) + (z // 2) * pair, pair), :, own_rows],
        init_piece,
        recv_sem.at[8],
    )
    init_copy.start()

    @pl.when(on_diagonal)
    def _():
        near(cache_ref, kvc.at[group], recv_sem.at[5]).start()

    @pl.when(jnp.logical_not(on_diagonal))
    def _():
        remote(
            cache_ref, kvc.at[group_of_partner(z, yh)], send_sem.at[5], recv_sem.at[5], group, t - core + yh
        ).start()

    def send_heads(src_ref, width, dst_ref, which):
        def body(k, carry):
            h = lax.rem(t + k, n_tp)
            to_ctx = 2 * z + lax.rem(h, 2)
            to_tp = (h // 2) * 2 + yh
            own = jnp.logical_and(to_ctx == c, to_tp == t)
            src = src_ref.at[:, columns(h, width)]
            dst = dst_ref.at[my_rows]

            @pl.when(own)
            def _():
                near(src, dst, recv_sem.at[which]).start()

            @pl.when(jnp.logical_not(own))
            def _():
                remote(src, dst, send_sem.at[which], recv_sem.at[which], to_ctx, to_tp).start()

            return carry

        lax.fori_loop(0, n_tp, body, 0)

    is_last = jnp.logical_and(t == n_tp - 1, yh == 1)
    conv_sem = recv_sem.at[jnp.where(is_last, 12, 0)]
    dt_width = steps.shape[1]
    per_dt = dt_width // n_heads

    def mixer_pieces(half, p):
        begin = p * conv_width
        return (
            (dt_ref.at[:, columns(p // per_dt, dt_width)], steps.at[plane_rows], 1),
            (
                conv_ref.at[:, pl.ds(pl.multiple_of(begin + half * half_width, 128), half_width)],
                chan.at[plane_rows, pl.ds(0, half_width)],
                0,
            ),
            (
                conv_ref.at[:, pl.ds(pl.multiple_of(begin + inner_width, 128), 2 * n_state)],
                chan.at[plane_rows, pl.ds(half_width, 2 * n_state)],
                0,
            ),
        )

    def gate_piece(half, p):
        return gate_ref.at[:, pl.ds(pl.multiple_of(p * inner_width + half * half_width, 128), half_width)]

    def plane_peer(k):
        return lax.rem(yh + lax.rem(k, 2), 2), lax.rem(t + k // 2, n_tp)

    def send_mixer(k, carry):
        half, p = plane_peer(k)
        for src, dst, which in mixer_pieces(half, p):
            to_sem = recv_sem.at[which] if which else conv_sem
            remote(src, dst, send_sem.at[which], to_sem, 2 * z + half, p).start()
        return carry

    def send_gate(k, carry):
        half, p = plane_peer(k)
        remote(
            gate_piece(half, p), gates.at[plane_rows], send_sem.at[4], recv_sem.at[4], 2 * z + half, p
        ).start()
        return carry

    send_heads(kv_ref, kv_width, raw_kv, 2)
    lax.fori_loop(1, 2 * n_tp, send_mixer, 0)
    for src, dst, which in mixer_pieces(yh, t):
        near(src, dst, recv_sem.at[which] if which else conv_sem).start()

    def region(buf, way, dist, parity, cut):
        slot = 2 * lax.rem(z - way * dist + nz, nz) + parity
        if not cut:
            return buf.at[slot]
        half = buf.shape[1] // 2
        return buf.at[slot, pl.ds(0 if way > 0 else half, half)]

    bufs = (kvc, kvp)

    def ring_copy(which, way, step, arriving):
        cut = step + 1 == far
        piece = region(bufs[which], way, step + 1 if arriving else step, core, cut)
        at = (which * 2 + (way < 0)) * far + step
        return remote(
            piece,
            piece,
            ring_send.at[at],
            ring_recv.at[at],
            2 * lax.rem(z + way + nz, nz) + yh,
            t,
        )

    def sib_copy(which, way, dist, arriving):
        cut = dist == far
        piece = region(bufs[which], way, dist, 1 - core if arriving else core, cut)
        at = (which * 2 + (way < 0)) * (far + 1) + dist
        return remote(piece, piece, sib_send.at[at], sib_recv.at[at], c, t + 1 - 2 * core)

    def ring_begin(which):
        for way in (1, -1):
            ring_copy(which, way, 0, False).start()
        sib_copy(which, 1, 0, False).start()

    def ring_advance(which, step):
        for way in (1, -1):
            ring_copy(which, way, step, True).wait_recv()
            if step + 1 < far:
                ring_copy(which, way, step + 1, False).start()
        for way in (1, -1):
            sib_copy(which, way, step + 1, False).start()

    def sib_wait(which, dist):
        for way in (1, -1) if dist else (1,):
            sib_copy(which, way, dist, True).wait_recv()

    wait_for(kvc.at[group], recv_sem.at[5])
    ring_begin(0)

    lane = lax.broadcasted_iota(jnp.int32, (rows, head), 1)
    sine = jnp.where(lane < head // 2, -sin_ref[...], sin_ref[...])
    cosine = cos_ref[...]

    def rotated(a):
        a = a.astype(F32)
        return (a * cosine + pltpu.roll(a, head // 2, 1) * sine).astype(BF16)

    wait_for(raw_kv, recv_sem.at[2])
    kvp[group] = jnp.concatenate([rotated(raw_kv[:, :head]), raw_kv[:, head:]], axis=1)
    ring_begin(1)

    first[...] = jnp.zeros(first.shape, F32)
    first[pl.ds(PAD - first_ref.shape[0], first_ref.shape[0]), :] = first_ref[...].astype(F32)
    small_ref[...] = jnp.zeros(small_ref.shape, F32)
    small_ref[0:1, 0:n_heads] = dt_bias_ref[...]
    small_ref[1:2, 0:n_heads] = rate_ref[...]
    small_ref[2:3, 0:n_heads] = skip_ref[...]
    half_heads = n_heads // 2
    to_lane = lax.broadcasted_iota(jnp.int32, (128, 128), 1)
    of_half = jnp.logical_and(
        lax.broadcasted_iota(jnp.int32, (128, 128), 0) == yh * half_heads + to_lane, to_lane < half_heads
    )
    small = exact_dot(small_ref[...], of_half.astype(F32))
    pick = lax.broadcasted_iota(jnp.int32, (dt_width, 128), 0) == (
        lax.rem(t, per_dt) * n_heads
        + yh * half_heads
        + lax.broadcasted_iota(jnp.int32, (dt_width, 128), 1)
    )
    row_at = lax.broadcasted_iota(jnp.int32, (rows, rows), 0)
    col_at = lax.broadcasted_iota(jnp.int32, (rows, rows), 1)
    causal = row_at >= col_at
    wide_at = 2 * 128
    wait_for(steps, recv_sem.at[1])
    raw_step = fast_dot(steps[...], pick.astype(F32).astype(BF16)) + small[0:1]
    step_size = jnp.maximum(raw_step, 0.0) + jnp.log1p(jnp.exp(-jnp.abs(raw_step)))
    log_decay = -jnp.exp(small[1:2]) * step_size
    tri = causal.astype(F32)
    cumulative = jnp.concatenate(
        [exact_dot(tri, log_decay[:rows]), exact_dot(tri, log_decay[rows:])], axis=0
    )
    cum_rows[...] = cumulative.T

    def spread_out(j, carry):
        cols = columns(j, wide_at)
        spread = lax.broadcasted_iota(jnp.int32, (128, wide_at), 0) == (
            j * (wide_at // phead) + lax.broadcasted_iota(jnp.int32, (128, wide_at), 1) // phead
        )
        spread = spread.astype(F32)
        for part in range(2):
            at = pl.ds(part * rows, rows)
            here = slice(part * rows, part * rows + rows)
            cum_here = exact_dot(cumulative[here], spread)
            step_here = exact_dot(step_size[here], spread)
            cum_wide[at, cols] = cum_here
            grown[at, cols] = jnp.exp(cum_here)
            step_wide[at, cols] = step_here
            toward_wide[at, cols] = step_here * jnp.exp(cum_here[rows - 1 : rows] - cum_here)
        skip_wide[:, cols] = exact_dot(small, spread)
        return carry

    lax.fori_loop(0, half_width // wide_at, spread_out, 0)
    ring_advance(0, 0)
    ring_advance(1, 0)

    last_rows = pl.ds(both_rows - PAD, PAD)
    wait_for(chan.at[last_rows], recv_sem.at[12])
    halo_copy = remote(
        chan.at[last_rows], halo, send_sem.at[6], recv_sem.at[6], 2 * lax.rem(z + 1, nz) + yh, t
    )
    halo_copy.start()
    wait_for(chan.at[pl.ds(0, both_rows - row_part)], recv_sem.at[0])
    send_heads(q_ref, q_width, raw_q, 3)
    halo_copy.wait_recv()
    n_taps = tap_ref.shape[0]
    piece = 256

    def convolve(j, carry):
        cols = columns(j, piece)
        begin = j * piece + jnp.where(j * piece < half_width, yh * half_width, inner_width - half_width)
        from_cols = pl.ds(pl.multiple_of(begin, 128), piece)
        before = jnp.where(z == 0, first[:, from_cols], halo[:, cols].astype(F32))
        wide = jnp.concatenate([before, chan[:, cols].astype(F32)], axis=0)
        total = bias_ref[from_cols][None, :]
        for tap in range(n_taps):
            start = PAD - (n_taps - 1) + tap
            total = total + tap_ref[pl.ds(tap, 1), from_cols] * wide[start : start + both_rows]
        mixed[:, cols] = silu(total)
        return carry

    lax.fori_loop(0, (half_width + n_state) // piece, convolve, 0)
    ring_advance(0, 1)
    in_cols = pl.ds(half_width, n_state)
    out_cols = pl.ds(half_width + n_state, n_state)

    def states(k, carry):
        j = lax.rem(k + z // far, half_width // wide_at)
        cols = columns(j, wide_at)
        fresh = []
        for part in range(2):
            at = pl.ds(part * rows, rows)
            here = mixed[at, cols]
            high, low = halves(here * step_wide[at, cols])
            x_high[at, cols] = high
            x_low[at, cols] = low
            toward = here * toward_wide[at, cols]
            fresh.append(exact_dot(mixed[at, in_cols], toward, (((0,), (0,)), ((), ()))))
        middle[:, cols] = fresh[0]
        later = grown[both_rows - 1 : both_rows, cols]
        fresh = later * fresh[0] + fresh[1]
        fresh = fresh.astype(BF16)
        decay = grown[rows - 1 : rows, cols] * later
        decay_1 = decay.astype(BF16).astype(F32)
        decay_2 = (decay - decay_1).astype(BF16).astype(F32)
        decay_3 = decay - decay_1 - decay_2
        at = lax.broadcasted_iota(jnp.int32, (PAD, wide_at), 0)
        decays = jnp.where(at == 0, decay_1, jnp.where(at == 1, decay_2, jnp.where(at == 2, decay_3, 0.0)))
        decays = decays.astype(BF16)
        for k in range(2 * wide_at // 128):
            i = j * (2 * wide_at // 128) + k
            lanes = slice(k // 2 * 128, k // 2 * 128 + 128)
            start = k % 2 * half_state
            state_out[i, :half_state] = fresh[start : start + half_state, lanes]
            state_out[i, half_state:] = decays[:, lanes]

            @pl.when(i == z)
            def _(i=i):
                near(state_out.at[i], state_all.at[z], recv_sem.at[7]).start()

            @pl.when(i != z)
            def _(i=i):
                remote(
                    state_out.at[i], state_all.at[z], send_sem.at[7], recv_sem.at[7], 2 * i + yh, t
                ).start()

        return carry

    lax.fori_loop(0, half_width // wide_at, states, 0)
    near(gate_piece(yh, t), gates.at[plane_rows], recv_sem.at[4]).start()
    lax.fori_loop(1, 2 * n_tp, send_gate, 0)
    ring_advance(1, 1)
    lax.fori_loop((half_width + n_state) // piece, own_width // piece, convolve, 0)

    for part in range(2):
        at = pl.ds(part * rows, rows)
        contact[part] = exact_dot(mixed[at, out_cols], mixed[at, in_cols], (((1,), (1,)), ((), ())))
    pair_lane = lax.broadcasted_iota(jnp.int32, (rows, 128), 1)
    pairs = half_width // 128

    def within(k, carry):
        part = k // pairs
        j = lax.rem(k, pairs)
        at = pl.ds(pl.multiple_of(part * rows, 16), rows)
        cols = columns(j, 128)
        cum_pair = cum_wide[at, cols]
        both = jnp.concatenate([x_high[at, cols], x_low[at, cols]], axis=1)
        pieces = []
        for i in range(2):
            row = cum_rows[pl.ds(2 * j + i, 1), :]
            row = jnp.where(part == 0, row[:, :rows], row[:, rows:])
            gap = cum_pair[:, i * phead : i * phead + 1] - row
            mixing = contact[part] * jnp.exp(jnp.where(causal, gap, HIDDEN))
            high, low = halves(mixing)
            product = fast_dot(high, both)
            pieces.append(product[:, :128] + product[:, 128:] + fast_dot(low, both[:, :128]))
        inner[at, cols] = mixed[at, cols] * skip_wide[2:3, cols] + jnp.where(
            pair_lane < phead, pieces[0], pieces[1]
        )
        return carry

    lax.fori_loop(0, 2 * pairs, within, 0)
    ring_advance(0, 2)

    wait_for(raw_q, recv_sem.at[3])
    mark = (lax.broadcasted_iota(jnp.int32, (rows, head), 1) == 0).astype(F32).astype(BF16)
    for h in range(local_q):
        part = rotated(raw_q[:, h * head : (h + 1) * head])
        queries[pl.ds(h * rows, rows), :] = jnp.concatenate([part, mark], axis=1)
    top[...] = jnp.full(top.shape, FLOOR, F32)
    acc[...] = jnp.zeros(acc.shape, F32)
    factor = math.log2(math.e) / math.sqrt(head)
    length = length_ref[0]
    pair_rows = 2 * cache_rows

    def update(key, value, diagonal):
        for h in range(local_q):
            at = pl.ds(h * rows, rows)
            score = fast_dot(queries[at, :], key, (((1,), (1,)), ((), ())))
            if diagonal:
                shape = (rows, 2 * rows)
                seen = lax.broadcasted_iota(jnp.int32, shape, 1) <= (
                    core * rows + lax.broadcasted_iota(jnp.int32, shape, 0)
                )
                masked = jnp.where(seen, score[:, pair_rows:], HIDDEN)
                score = jnp.concatenate([score[:, :pair_rows], masked], axis=1)
            old = top[at, :]
            new = jnp.maximum(old, jnp.max(score, axis=1, keepdims=True))
            top[at, :] = new
            weight = jnp.exp2((score - widened(new, score.shape[1])) * factor)
            scale = jnp.exp2((old - new) * factor)
            acc[at, :] = acc[at, :] * widened(scale, 2 * head) + fast_dot(weight.astype(BF16), value)

    def attend(place):
        def run(prompt, diagonal):
            lanes = lax.broadcasted_iota(jnp.int32, (pair_rows, head), 1)
            slots = place * pair_rows + lax.broadcasted_iota(jnp.int32, (pair_rows, head), 0)
            hide = jnp.where(jnp.logical_and(lanes == 0, slots >= length), HIDDEN, 0.0).astype(BF16)
            cached = kvc[pl.ds(2 * place, 2)].reshape(pair_rows, 2 * head)
            key, value = cached[:, :head], cached[:, head:]
            if prompt:
                more = kvp[pl.ds(2 * place, 2)].reshape(2 * rows, 2 * head)
                key = jnp.concatenate([key, more[:, :head]], axis=0)
                value = jnp.concatenate([value, more[:, head:]], axis=0)
                hide = jnp.concatenate([hide, jnp.zeros((2 * rows, head), BF16)], axis=0)
            ones = jnp.ones(value.shape, BF16)
            update(
                jnp.concatenate([key, hide], axis=1), jnp.concatenate([value, ones], axis=1), diagonal
            )

        pl.when(place < z)(functools.partial(run, True, False))
        pl.when(place == z)(functools.partial(run, True, True))
        pl.when(place > z)(functools.partial(run, False, False))

    def pass_states():
        wait_for(state_all, recv_sem.at[7])
        init_copy.wait()

        def scan_group(i, state):
            enter_out[i] = state.astype(BF16)
            parts = state_all[i, half_state:].astype(F32)
            decay = parts[0:1] + parts[1:2] + parts[2:3]
            return decay * state + state_all[i, :half_state].astype(F32)

        lax.fori_loop(0, nz, scan_group, init_piece[...].reshape(128, half_state).T)

        def send_enter(k, carry):
            i = lax.rem(z + k, nz)
            remote(
                enter_out.at[i],
                enter_all.at[own_rows, own_cols],
                send_sem.at[9],
                recv_sem.at[9],
                2 * i + yh,
                t,
            ).start()
            return carry

        near(enter_out.at[z], enter_all.at[own_rows, own_cols], recv_sem.at[9]).start()
        lax.fori_loop(1, nz, send_enter, 0)

    block = rows // 2
    square_copy = remote(square_out, square_in, send_sem.at[12], recv_sem.at[13], 2 * z + 1 - yh, t)

    def end_mixer():
        wait_for(enter_all, recv_sem.at[9])
        wait_for(gates, recv_sem.at[4])
        mid_high, mid_low = halves(grown[rows - 1 : rows, :] * enter_all[...].astype(F32) + middle[...])
        next_high[...] = mid_high
        next_low[...] = mid_low

        def gate_rows(k, carry):
            at = pl.ds(pl.multiple_of(k * block, 16), block)
            out_high, out_low = halves(mixed[at, out_cols])

            def close(carried):
                y = inner[at, :] + grown[at, :] * carried
                gated = y * silu(gates[at, :].astype(F32))
                inner[at, :] = gated
                square = jnp.sum(gated * gated, axis=1, keepdims=True)
                squares[at, :] = jnp.broadcast_to(square, (block, 128))

            @pl.when(k < 2)
            def _():
                close(fast_dot(out_high, enter_all[...]) + fast_dot(out_low, enter_all[...]))

            @pl.when(k >= 2)
            def _():
                first_part = fast_dot(out_high, next_high[...]) + fast_dot(out_low, next_high[...])
                close(first_part + fast_dot(out_high, next_low[...]))

            return carry

        lax.fori_loop(0, 4, gate_rows, 0)
        square_out[...] = squares[...].T[:8]
        square_copy.start()

    def send_mixed():
        square_copy.wait_recv()
        total = square_out[0:1, :] + square_in[0:1, :]
        norm_row = lax.rsqrt(total / inner_width + 1e-05)
        squares[...] = jnp.broadcast_to(norm_row, (128, both_rows)).T
        out_at = pl.ds(pl.multiple_of(t * inner_width + yh * half_width, 128), half_width)
        gain = gain_ref[:, pl.ds(pl.multiple_of(yh * half_width, 128), half_width)]

        def normed(k, carry):
            part = lax.rem(k + 2 * yh, 4)
            at = pl.ds(pl.multiple_of(part * block, 16), block)
            mamba_loc[at, :] = (inner[at, :] * widened(squares[at, :], half_width) * gain).astype(BF16)
            return carry

        lax.fori_loop(0, 4, normed, 0)

        def send_mamba(k, carry):
            half, p = plane_peer(k)
            src = mamba_loc.at[pl.ds(pl.multiple_of(half * rows + p * row_part, 16), row_part)]
            remote(src, mamba_ref.at[:, out_at], send_sem.at[11], recv_sem.at[11], 2 * z + half, p).start()
            return carry

        lax.fori_loop(1, 2 * n_tp, send_mamba, 0)
        near(mamba_loc.at[plane_rows], mamba_ref.at[:, out_at], recv_sem.at[11]).start()

    def sib_wait_both(dist):
        sib_wait(0, dist)
        sib_wait(1, dist)

    events = {
        0: (functools.partial(sib_wait_both, 0), functools.partial(sib_wait_both, 1)),
        1: (pass_states,),
        2: (functools.partial(ring_advance, 1, 2),),
        3: (functools.partial(sib_wait_both, 2), functools.partial(ring_advance, 0, 3)),
        5: (functools.partial(sib_wait_both, 3), end_mixer),
        6: (functools.partial(ring_advance, 1, 3), send_mixed),
        7: (functools.partial(sib_wait_both, 4),),
    }

    def attend_next(k, carry):
        for at, calls in events.items():

            @pl.when(k == at)
            def _(calls=calls):
                for call in calls:
                    call()

        back = lax.rem(k, 2) == 0
        attend(lax.rem(jnp.where(back, z + nz - k // 2, z + (k + 1) // 2), nz))
        return carry

    lax.fori_loop(0, nz, attend_next, 0)
    for h in range(local_q):
        found = acc[pl.ds(h * rows, rows), :]
        attn_loc[:, h * head : (h + 1) * head] = (found[:, :head] / found[:, head:]).astype(BF16)

    def send_attn(k, carry):
        p = lax.rem(t + k, n_tp)
        src = attn_loc.at[pl.ds(pl.multiple_of(p * row_part, 16), row_part)]
        dst = attn_ref.at[:, columns(t - core + yh, q_width)]
        own = jnp.logical_and(group == c, p == t)

        @pl.when(own)
        def _():
            near(src, dst, recv_sem.at[10]).start()

        @pl.when(jnp.logical_not(own))
        def _():
            remote(src, dst, send_sem.at[10], recv_sem.at[10], group, p).start()

        return carry

    lax.fori_loop(0, n_tp, send_attn, 0)

    wait_for(attn_ref, recv_sem.at[10])
    wait_for(mamba_ref, recv_sem.at[11])
    others = (n_tp - 1) * row_part
    plane_others = pl.ds(0, both_rows - row_part)
    wait_for(chan.at[plane_others], send_sem.at[0])
    wait_for(steps.at[plane_others], send_sem.at[1])
    wait_for(gates.at[plane_others], send_sem.at[4])
    wait_for(mamba_loc.at[plane_others], send_sem.at[11])
    square_copy.wait_send()
    for ref, which in ((raw_kv, 2), (raw_q, 3), (attn_loc, 10)):

        @pl.when(on_diagonal)
        def _(ref=ref, which=which):
            wait_for(ref.at[pl.ds(0, others)], send_sem.at[which])

        @pl.when(jnp.logical_not(on_diagonal))
        def _(ref=ref, which=which):
            wait_for(ref, send_sem.at[which])

    @pl.when(jnp.logical_not(on_diagonal))
    def _():
        wait_for(cache_ref, send_sem.at[5])

    halo_copy.wait_send()
    wait_for(state_all.at[pl.ds(0, nz - 1)], send_sem.at[7])
    wait_for(enter_out.at[pl.ds(0, nz - 1)], send_sem.at[9])
    for which in range(2):
        for way in (1, -1):
            for step in range(far):
                ring_copy(which, way, step, False).wait_send()
        sib_copy(which, 1, 0, False).wait_send()
        for dist in range(1, far + 1):
            for way in (1, -1):
                sib_copy(which, way, dist, False).wait_send()


def group_of_partner(z, yh):
    return 2 * z + yh


def local(
    queries,
    keyvals,
    cache_kv,
    conv_input,
    gate_input,
    dt_raw,
    conv_weight,
    conv_bias,
    dt_bias,
    decay_log,
    skip_weight,
    norm_gain,
    ssm_init,
    conv_init,
    prompt_start,
    cache_length,
):
    n_ctx = lax.axis_size("ctx")
    n_tp = lax.axis_size("tp")
    c = lax.axis_index("ctx")
    t = lax.axis_index("tp")
    head = cache_kv.shape[1] // 2
    row_part = queries.shape[0]
    rows = row_part * n_tp
    n_heads, phead, n_state = ssm_init.shape
    inner_width = n_heads * phead
    conv_width = conv_weight.shape[1]
    q_width = queries.shape[1] // n_tp
    cache_rows = cache_kv.shape[0]
    far = n_ctx // 4
    half = inner_width // 2
    own_width = half + 2 * n_state

    group = (c // 2) * 2 + t % 2
    half_width = head // 2
    lane_index = (jnp.arange(head, dtype=jnp.int32) % half_width).astype(F32)
    inverse = jnp.power(F32(10000.0), -lane_index / half_width)
    positions = prompt_start[0] + group * rows + jnp.arange(rows, dtype=jnp.int32)
    angles = positions.astype(F32)[:, None] * inverse[None, :]
    hbm = pl.BlockSpec(memory_space=pl.ANY)
    vmem = pl.BlockSpec(memory_space=pltpu.VMEM)
    smem = pl.BlockSpec(memory_space=pltpu.SMEM)
    dma = pltpu.SemaphoreType.DMA
    local_rows = rows * q_width // head
    return pl.pallas_call(
        functools.partial(kernel, n_ctx, n_tp, phead),
        out_shape=(
            jax.ShapeDtypeStruct(queries.shape, BF16),
            jax.ShapeDtypeStruct(gate_input.shape, BF16),
        ),
        in_specs=[smem] + [hbm] * 7 + [vmem] * 9,
        out_specs=(hbm, hbm),
        scratch_shapes=[
            pltpu.VMEM((n_ctx, cache_rows, 2 * head), BF16),
            pltpu.VMEM((n_ctx, rows, 2 * head), BF16),
            pltpu.VMEM((rows, 2 * head), BF16),
            pltpu.VMEM((rows, q_width), BF16),
            pltpu.VMEM((2 * rows, own_width), BF16),
            pltpu.VMEM((PAD, own_width), BF16),
            pltpu.VMEM((2 * rows, half), BF16),
            pltpu.VMEM((2 * rows, min(128, dt_raw.shape[1])), BF16),
            pltpu.VMEM((2 * rows, own_width), F32),
            pltpu.VMEM((2 * rows, half), BF16),
            pltpu.VMEM((2 * rows, half), BF16),
            pltpu.VMEM((2 * rows, half), F32),
            pltpu.VMEM((2 * rows, half), F32),
            pltpu.VMEM((2 * rows, half), F32),
            pltpu.VMEM((2 * rows, half), F32),
            pltpu.VMEM((2 * rows, half), F32),
            pltpu.VMEM((8, half), F32),
            pltpu.VMEM((128, 2 * rows), F32),
            pltpu.VMEM((2, rows, rows), F32),
            pltpu.VMEM((n_ctx // 2, n_state // 2 + PAD, 128), BF16),
            pltpu.VMEM((n_ctx // 2, n_state // 2 + PAD, 128), BF16),
            pltpu.VMEM((n_ctx // 2, n_state // 2, 128), BF16),
            pltpu.VMEM((n_state, half), BF16),
            pltpu.VMEM((local_rows, 2 * head), BF16),
            pltpu.VMEM((local_rows, 128), F32),
            pltpu.VMEM((local_rows, 2 * head), F32),
            pltpu.VMEM((rows, q_width), BF16),
            pltpu.VMEM((2 * rows, half), BF16),
            pltpu.VMEM((PAD, conv_width), F32),
            pltpu.VMEM((8, 128), F32),
            pltpu.VMEM((128 // phead, phead, n_state // 2), F32),
            pltpu.VMEM((n_state, half), F32),
            pltpu.VMEM((n_state, half), BF16),
            pltpu.VMEM((n_state, half), BF16),
            pltpu.VMEM((2 * rows, 128), F32),
            pltpu.VMEM((8, 2 * rows), F32),
            pltpu.VMEM((8, 2 * rows), F32),
            dma((13,)),
            dma((14,)),
            dma((4 * far,)),
            dma((4 * far,)),
            dma((4 * (far + 1),)),
            dma((4 * (far + 1),)),
        ],
        compiler_params=pltpu.CompilerParams(
            collective_id=0, has_side_effects=True, vmem_limit_bytes=62 * 1024 * 1024
        ),
        cost_estimate=pl.CostEstimate(
            flops=8 * 10**9, bytes_accessed=6 * 10**6, transcendentals=14 * 10**6
        ),
    )(
        cache_length,
        queries,
        keyvals,
        cache_kv,
        conv_input,
        gate_input,
        dt_raw,
        ssm_init,
        conv_init,
        conv_weight,
        conv_bias,
        dt_bias[None, :],
        decay_log[None, :],
        skip_weight[None, :],
        norm_gain[None, :],
        jnp.cos(angles),
        jnp.sin(angles),
    )


def solution(mesh):
    return jax.shard_map(
        local,
        mesh=mesh,
        in_specs=(
            P(("ctx", "tp"), None),
            P(("ctx", "tp"), None),
            P("ctx", "tp"),
            P(("ctx", "tp"), None),
            P(("ctx", "tp"), None),
            P(("ctx", "tp"), None),
            P(None, "tp"),
            P("tp"),
            P("tp"),
            P("tp"),
            P("tp"),
            P("tp"),
            P("tp", None, None),
            P(None, "tp"),
            P(),
            P(),
        ),
        out_specs=(P(("ctx", "tp"), None), P(("ctx", "tp"), None)),
        check_vma=False,
    )
```
